128 devices in a mesh: dp: 16 (over x, y), mp: 8 (over z, core).
Axes of the slice: x: 4, y: 4, z: 4, core: 2. Of those that a mesh axis runs over, the one named last changes fastest.
Arguments:
- grad_parts: bfloat16 [16, 3, 4096, 4096], P('dp', None, 'mp')
- moment: float32 [3, 4096, 4096], P(None, ('mp', 'dp'))
- left_roots: bfloat16 [128, 1024, 1024], P(('dp', 'mp'))
- right_roots: bfloat16 [128, 1024, 1024], P(('dp', 'mp'))
- block_owner: int32 [48], replicated, may hold values from 0 to 127, as said below
Outputs:
- update: bfloat16 [128, 1024, 1024], P(('dp', 'mp'))
The draws below stay inside these ranges and needn't reach their ends.
Inputs may be any that keep to these rules, and one draw needn't show every extreme that they name: `block_owner`: each device owns at most 1 block and some device owns exactly 1; a block's factors sit in its owner's slots in the order of block numbers; slots without a block hold factors that are not used.
All inputs are finite; a program needn't handle non-finite values.
Results may differ from the reference program's by a relative error of at most 0.02.
Values may be sent and summed in bfloat16 or wider, within the bound.
No kernel may reach another device: no remote copies, remote signals or barrier semaphores. Data moves between devices by JAX's collectives and lax.ppermute only.
A program may use at most 128 MiB of HBM per device.

```python
import math
import jax
import jax.numpy as jnp
from jax import lax

D = 4096
BS = 1024
MATS = 3
NR = 4
NBLK = 48
CAP = 1
SLOTS = 128
N_DP = 16
DEVICES = 128


def draw_grad_parts(key, part):
    key = jax.random.fold_in(key, 11)
    key_rows, key_cols, key_base = jax.random.split(key, 3)
    within = (jnp.arange(D) % BS).astype(jnp.float32) / BS
    row_scale = jnp.exp(math.log(3.0) * within)[None, :, None] * jnp.exp(0.5 * math.log(10.0) * jax.random.uniform(key_rows, (MATS, D, 1), jnp.float32))
    col_scale = jnp.exp(0.5 * math.log(10.0) * jax.random.uniform(key_cols, (MATS, 1, D), jnp.float32))
    base = jax.random.normal(key_base, (N_DP, MATS, D, D), jnp.float32)
    return (0.25 * base * (row_scale * col_scale)[None]).astype(jnp.bfloat16)


def draw_moment(key, part):
    key = jax.random.fold_in(key, 12)
    key_block, key_entry = jax.random.split(key)
    block_scale = jnp.exp(jax.random.uniform(key_block, (MATS, NR, 1, NR, 1), jnp.float32, math.log(0.1), math.log(10.0)))
    entry = jnp.exp(jax.random.uniform(key_entry, (MATS, NR, BS, NR, BS), jnp.float32, math.log(0.5), math.log(2.0)))
    return (block_scale * entry).reshape(MATS, D, D).astype(jnp.float32)


def dominant(key_diagonal, noise_part):
    diagonal = jnp.exp(jax.random.uniform(key_diagonal, (SLOTS, BS), jnp.float32, math.log(0.5), math.log(3.0)))
    symmetric = (noise_part + jnp.swapaxes(noise_part, 1, 2)) * (0.4 / math.sqrt(2.0 * BS))
    return (symmetric + jnp.eye(BS, dtype=jnp.float32)[None] * diagonal[:, None, :]).astype(jnp.bfloat16)


def draw_left_roots(key, part):
    key = jax.random.fold_in(key, 13)
    key_diagonal, key_noise = jax.random.split(key)
    noise_part = jax.random.normal(key_noise, (SLOTS, BS, BS), jnp.float32)
    return dominant(key_diagonal, noise_part)


def draw_right_roots(key, part):
    key = jax.random.fold_in(key, 14)
    key_diagonal, key_noise = jax.random.split(key)
    noise_part = jax.random.normal(key_noise, (SLOTS, BS, BS), jnp.float32)
    return dominant(key_diagonal, noise_part)


def draw_block_owner(key, part):
    key = jax.random.fold_in(key, 15)
    key_devices, key_order = jax.random.split(key)
    shuffled = jax.random.permutation(key_devices, DEVICES).astype(jnp.int32)
    positions = jnp.arange(NBLK, dtype=jnp.int32)
    listed = shuffled[positions % DEVICES]
    return jax.random.permutation(key_order, listed).astype(jnp.int32)


def setup_inputs(seed: int = 0) -> dict:
    key_list = jax.random.split(jax.random.key(seed), 6)
    return {
        "grad_parts": draw_grad_parts(jax.random.fold_in(key_list[5], 71), 0),
        "moment": draw_moment(jax.random.fold_in(key_list[5], 71), 0),
        "left_roots": draw_left_roots(jax.random.fold_in(key_list[5], 71), 0),
        "right_roots": draw_right_roots(jax.random.fold_in(key_list[5], 71), 0),
        "block_owner": draw_block_owner(jax.random.fold_in(key_list[5], 71), 0),
    }


BETA_TWO = 0.999
ADAM_EPS = 1e-08
NORM_EPS = 1e-06

def slot_tables(block_owner, capacity, slot_count):
    block_total = block_owner.shape[0]
    numbers = jnp.arange(block_total, dtype=jnp.int32)
    earlier = (block_owner[:, None] == block_owner[None, :]) & (numbers[None, :] < numbers[:, None])
    ranking = lax.optimization_barrier(jnp.sum(earlier.astype(jnp.int32), axis=1))
    slot_key = (block_owner * capacity + ranking).astype(jnp.int32)
    queries = jnp.arange(slot_count, dtype=jnp.int32)
    matches = (queries[:, None] == slot_key[None, :]).astype(jnp.int32)
    present = lax.optimization_barrier(jnp.sum(matches, axis=1))
    block_of = lax.optimization_barrier(jnp.sum(matches * numbers[None, :], axis=1)).astype(jnp.int32)
    return (slot_key, block_of, present)

def reference(grad_parts, moment, left_roots, right_roots, block_owner):
    gradient = grad_parts[0].astype(jnp.float32)
    for member in range(1, N_DP):
        gradient = gradient + grad_parts[member].astype(jnp.float32)
    second = BETA_TWO * moment + (1.0 - BETA_TWO) * gradient * gradient
    adam_dir = gradient / (jnp.sqrt(second) + ADAM_EPS)
    block_power_adam = lax.optimization_barrier(jnp.sum((adam_dir * adam_dir).reshape(MATS, NR, BS, NR, BS), axis=(2, 4))).reshape(NBLK)
    blocks = gradient.astype(jnp.bfloat16).reshape(MATS, NR, BS, NR, BS).transpose(0, 1, 3, 2, 4).reshape(NBLK, BS, BS)
    slot_key, block_of, present = slot_tables(block_owner, CAP, SLOTS)

    def precondition(number):
        where_slot = slot_key[number]
        left_one = lax.dynamic_index_in_dim(left_roots, where_slot, 0, keepdims=False)
        right_one = lax.dynamic_index_in_dim(right_roots, where_slot, 0, keepdims=False)
        grad_block = lax.dynamic_index_in_dim(blocks, number, 0, keepdims=False)
        first_step = jnp.dot(left_one, grad_block, preferred_element_type=jnp.float32).astype(jnp.bfloat16)
        shaped = jnp.dot(first_step, right_one, preferred_element_type=jnp.float32)
        block_power = jnp.sum(shaped * shaped)
        adam_power = lax.dynamic_index_in_dim(block_power_adam, number, 0, keepdims=False)
        return (shaped * (jnp.sqrt(adam_power) * lax.rsqrt(block_power + NORM_EPS))).astype(jnp.bfloat16)
    grafted = lax.map(precondition, jnp.arange(NBLK, dtype=jnp.int32))
    update = jnp.zeros((SLOTS, BS, BS), jnp.bfloat16).at[slot_key].set(grafted)
    return update
```

```python
import jax
import jax.numpy as jnp
from jax import lax
from jax.sharding import PartitionSpec as P

BETA_TWO = 0.999
ADAM_EPS = 1e-08
NORM_EPS = 1e-06
SIDE = 4
CHUNKS = 2
LANES = 128


def device_number(x, y, z, core):
    return ((x * SIDE + y) * SIDE + z) * 2 + core


def shifted(axis, sign):
    pairs = []
    for x in range(SIDE):
        for y in range(SIDE):
            for z in range(SIDE):
                for core in range(2):
                    place = [x, y]
                    place[axis] = (place[axis] + (sign if core else -sign)) % SIDE
                    pairs.append((device_number(x, y, z, core), device_number(*place, z, core)))
    return pairs


def send(value, axis, sign):
    return lax.ppermute(value, ("dp", "mp"), shifted(axis, sign))


def reduce_axis(piece, position, step, axis):
    wide = lambda value: value.astype(jnp.float32)
    far = send(piece((position + 2) % SIDE), axis, 1)
    near = send(piece((position - step) % SIDE), axis, -1)
    joined = (wide(piece((position + step) % SIDE)) + wide(far)).astype(jnp.bfloat16)
    joined = send(joined, axis, 1)
    return wide(piece(position)) + wide(near) + wide(joined)


def slot_blocks(block_owner, slot_count):
    numbers = jnp.arange(block_owner.shape[0], dtype=jnp.int32)
    queries = jnp.arange(slot_count, dtype=jnp.int32)
    matches = (queries[:, None] == block_owner[None, :]).astype(jnp.int32)
    return jnp.sum(matches * numbers[None, :], axis=1), jnp.sum(matches, axis=1)


def shards(grad_parts, moment, left_roots, right_roots, block_owner):
    dp_count = lax.axis_size("dp")
    mp_count = lax.axis_size("mp")
    dp_index = lax.axis_index("dp")
    mp_index = lax.axis_index("mp")
    matrices = grad_parts.shape[1]
    width = grad_parts.shape[3]
    block = left_roots.shape[1]
    sides = width // block
    x, y = dp_index // SIDE, dp_index % SIDE
    step = 2 * (mp_index % 2) - 1
    rows = moment.shape[1] // CHUNKS
    half = width // 2
    parts = grad_parts[0].reshape(matrices, SIDE, SIDE, CHUNKS, rows, width)

    block_of, present = slot_blocks(block_owner, dp_count * mp_count)
    mine = block_of.reshape(dp_count, mp_count)[:, mp_index]
    source = 2 * (mine // sides % sides)
    column = mine // (sides * sides) * sides + mine % sides
    picks = ((source[:, None] + jnp.arange(2)[None, :]) * (matrices * sides) + column[:, None]).reshape(-1)
    own_present = present[dp_index * mp_count + mp_index] > 0

    received = []
    for chunk in range(CHUNKS):
        sums = []
        for first in (0, 1):
            here = (x, y)[first]
            there = (x, y)[1 - first]
            cut = parts[:, :, :, chunk, :, first * half : (first + 1) * half]

            def piece(j, cut=cut, first=first):
                return lax.dynamic_index_in_dim(cut, j, 1 + first, keepdims=False)

            partial = reduce_axis(piece, here, step, first).astype(jnp.bfloat16)

            def inner(j, partial=partial):
                return lax.dynamic_index_in_dim(partial, j, 1, keepdims=False)

            sums.append(reduce_axis(inner, there, step, 1 - first))
        pieces = []
        for matrix in range(matrices):
            for side in range(sides):
                first, offset = divmod(side * block, half)
                gradient = sums[first][matrix, :, offset : offset + block]
                known = moment[matrix, chunk * rows : (chunk + 1) * rows, side * block : (side + 1) * block]
                second = BETA_TWO * known + (1.0 - BETA_TWO) * gradient * gradient
                direction = gradient / (jnp.sqrt(second) + ADAM_EPS)
                square = direction * direction
                power = sum(square[:, k : k + LANES] for k in range(0, block, LANES))
                pieces.append(jnp.concatenate([gradient, power], axis=1).astype(jnp.bfloat16))
        gathered = lax.all_gather(jnp.stack(pieces), "mp", axis=0, tiled=True)
        outgoing = jnp.take(gathered, picks, axis=0, mode="clip")
        outgoing = outgoing.reshape(dp_count, 2, rows, block + LANES)
        received.append(lax.all_to_all(outgoing, "dp", 0, 0, tiled=True))
    together = jnp.stack(received, axis=2)
    adam_power = jnp.sum(together[..., block:].astype(jnp.float32))
    grad_block = together[..., :block].transpose(1, 0, 2, 3, 4).reshape(block, block)
    first_step = jnp.dot(left_roots[0], grad_block, preferred_element_type=jnp.float32).astype(jnp.bfloat16)
    shaped = jnp.dot(first_step, right_roots[0], preferred_element_type=jnp.float32)
    block_power = jnp.sum(shaped * shaped)
    grafted = shaped * (jnp.sqrt(adam_power) * lax.rsqrt(block_power + NORM_EPS))
    return jnp.where(own_present, grafted, 0.0).astype(jnp.bfloat16)[None]


def solution(mesh):
    placed = (
        P("dp", None, "mp", None),
        P(None, ("mp", "dp"), None),
        P(("dp", "mp"), None, None),
        P(("dp", "mp"), None, None),
        P(),
    )
    return jax.shard_map(
        shards, mesh=mesh, in_specs=placed, out_specs=P(("dp", "mp"), None, None), check_vma=False
    )
```

```python
import functools

import jax
import jax.numpy as jnp
from jax import lax
from jax.experimental import pallas as pl
from jax.experimental.pallas import tpu as pltpu
from jax.sharding import PartitionSpec as P

BETA_TWO = 0.999
ADAM_EPS = 1e-08
NORM_EPS = 1e-06
SIDE = 4
CHUNKS = 2
LANES = 128
VMEM_LIMIT = 48 * 1024 * 1024
F32 = jnp.float32
BF16 = jnp.bfloat16


def device_number(x, y, z, core):
    return ((x * SIDE + y) * SIDE + z) * 2 + core


def routes(move):
    pairs = []
    for x in range(SIDE):
        for y in range(SIDE):
            for z in range(SIDE):
                for core in range(2):
                    dx, dy, dz, swap = move(core)
                    target = device_number((x + dx) % SIDE, (y + dy) % SIDE, (z + dz) % SIDE, core ^ swap)
                    pairs.append((device_number(x, y, z, core), target))
    return pairs


def send(value, move):
    return lax.ppermute(value, ("dp", "mp"), routes(move))


def in_plane(phase, sign):
    return lambda core: (sign, 0, 0, 0) if core == phase else (0, sign, 0, 0)


def wide(value):
    return value.astype(F32)


def call(kernel, out_shape, grid, in_specs, out_specs, scratch=(), cost=1 << 20):
    return pl.pallas_call(
        kernel,
        out_shape=out_shape,
        grid_spec=pltpu.PrefetchScalarGridSpec(
            num_scalar_prefetch=1, grid=grid, in_specs=in_specs, out_specs=out_specs, scratch_shapes=list(scratch)
        ),
        compiler_params=pltpu.CompilerParams(vmem_limit_bytes=VMEM_LIMIT),
        cost_estimate=pl.CostEstimate(flops=cost, bytes_accessed=4 * cost, transcendentals=0),
    )


def row_block(ids, j, q):
    j, q = lax.rem(j + 2 * SIDE, SIDE), lax.rem(q + 2 * SIDE, SIDE)
    return jnp.where(ids[2] == 0, j * SIDE + q, q * SIDE + j)


def grads_spec(m, rows, half, chunk, offset, column, ahead=0):
    def index(t, ids):
        q = t if not ahead else lax.rem(ids[1] + ahead + t, SIDE)
        return 0, row_block(ids, ids[0] + offset, q), chunk, 0, column

    return pl.BlockSpec((m, 1, 1, rows, half), index)


def extract(ids, parts, chunk):
    m, _, _, rows, width = parts.shape
    half = width // 2

    def kernel(ids, a, b, c, d, up, down):
        up[0, :, 0] = a[:, 0, 0]
        up[1, :, 0] = b[:, 0, 0]
        down[0, :, 0] = c[:, 0, 0]
        down[1, :, 0] = d[:, 0, 0]

    spec = functools.partial(grads_spec, m, rows, half, chunk)
    out = jax.ShapeDtypeStruct((2, m, SIDE, rows, half), BF16)
    out_spec = pl.BlockSpec((2, m, 1, rows, half), lambda t, ids: (0, 0, t, 0, 0))
    return call(
        kernel,
        [out, out],
        (SIDE,),
        [spec(2, 1), spec(1, 0), spec(-2, 0), spec(-1, 1)],
        [out_spec, out_spec],
    )(ids, parts, parts, parts, parts)


def relay(ids, parts, from_up, from_down, chunk):
    m, _, _, rows, width = parts.shape
    half = width // 2

    def kernel(ids, a, b, below, above, up, down):
        up[:, 0] = (wide(a[:, 0, 0]) + wide(below[0, :, 0])).astype(BF16)
        down[:, 0] = (wide(b[:, 0, 0]) + wide(above[0, :, 0])).astype(BF16)

    spec = functools.partial(grads_spec, m, rows, half, chunk)
    out = jax.ShapeDtypeStruct((m, SIDE, rows, half), BF16)
    out_spec = pl.BlockSpec((m, 1, rows, half), lambda t, ids: (0, t, 0, 0))
    got = pl.BlockSpec((1, m, 1, rows, half), lambda t, ids: (0, 0, t, 0, 0))
    return call(kernel, [out, out], (SIDE,), [spec(1, 1), spec(-1, 0), got, got], [out_spec, out_spec])(
        ids, parts, parts, from_down, from_up
    )


def first_sum(ids, parts, from_up, from_down, late_up, late_down, chunk):
    m, _, _, rows, width = parts.shape
    half = width // 2

    def kernel(ids, own, below, above, late_above, late_below, total, up, down):
        t = pl.program_id(0)
        left = (wide(own[:, 0, 0, :, :half]) + wide(below[0, :, 0]) + wide(late_above[:, 0])).astype(BF16)
        right = (wide(own[:, 0, 0, :, half:]) + wide(above[0, :, 0]) + wide(late_below[:, 0])).astype(BF16)
        total[:, 0, :, :half] = left
        total[:, 0, :, half:] = right

        @pl.when(t == 0)
        def _():
            up[1] = left

        @pl.when(t == 1)
        def _():
            up[0] = right
            down[0] = left

        @pl.when(t == 2)
        def _():
            down[1] = right

    def at(t, ids):
        return lax.rem(ids[1] + 1 + t, SIDE)

    got = pl.BlockSpec((1, m, 1, rows, half), lambda t, ids: (1, 0, at(t, ids), 0, 0))
    late = pl.BlockSpec((m, 1, rows, half), lambda t, ids: (0, at(t, ids), 0, 0))
    whole = pl.BlockSpec((2, m, rows, half), lambda t, ids: (0, 0, 0, 0))
    return call(
        kernel,
        [jax.ShapeDtypeStruct((m, SIDE, rows, width), BF16)] + [jax.ShapeDtypeStruct((2, m, rows, half), BF16)] * 2,
        (SIDE,),
        [grads_spec(m, rows, width, chunk, 0, 0, ahead=1), got, got, late, late],
        [pl.BlockSpec((m, 1, rows, width), lambda t, ids: (0, at(t, ids), 0, 0)), whole, whole],
    )(ids, parts, from_down, from_up, late_up, late_down)


def second_relay(ids, total, from_up, from_down):
    m, _, rows, width = total.shape
    half = width // 2

    def kernel(ids, a, b, below, above, up, down):
        up[...] = (wide(a[:, 0]) + wide(below[0])).astype(BF16)
        down[...] = (wide(b[:, 0]) + wide(above[0])).astype(BF16)

    def spec(offset, column):
        return pl.BlockSpec(
            (m, 1, rows, half), lambda t, ids: (0, lax.rem(ids[1] + offset + SIDE, SIDE), 0, column)
        )

    out = jax.ShapeDtypeStruct((m, rows, half), BF16)
    out_spec = pl.BlockSpec((m, rows, half), lambda t, ids: (0, 0, 0))
    got = pl.BlockSpec((1, m, rows, half), lambda t, ids: (0, 0, 0, 0))
    return call(kernel, [out, out], (1,), [spec(1, 1), spec(-1, 0), got, got], [out_spec, out_spec])(
        ids, total, total, from_down, from_up
    )


def second_sum(ids, total, from_up, from_down, late_up, late_down, moment, chunk, block):
    m, _, rows, width = total.shape
    half = width // 2
    sides = width // block

    def kernel(ids, own, below, above, late_above, late_below, known, out):
        for side in range(sides):
            at = side * block
            here = slice(at % half, at % half + block)
            raw, late = (below, late_above) if at < half else (above, late_below)
            power = jnp.zeros((rows, LANES), F32)
            for k in range(at, at + block, LANES):
                piece = slice(k % half, k % half + LANES)
                gradient = wide(own[0, 0, :, k : k + LANES]) + wide(raw[0, 0, :, piece]) + wide(late[0, :, piece])
                second = BETA_TWO * known[0, 0, :, k : k + LANES] + (1.0 - BETA_TWO) * gradient * gradient
                direction = gradient / (jnp.sqrt(second) + ADAM_EPS)
                power = power + direction * direction
                out[side, :, k - at : k - at + LANES] = gradient.astype(BF16)
            out[side, :, block:] = power.astype(BF16)

    half_spec = pl.BlockSpec((1, rows, half), lambda t, ids: (t, 0, 0))
    got = pl.BlockSpec((1, 1, rows, half), lambda t, ids: (1, t, 0, 0))
    return call(
        kernel,
        jax.ShapeDtypeStruct((m * sides, rows, block + LANES), BF16),
        (m,),
        [
            pl.BlockSpec((1, 1, rows, width), lambda t, ids: (t, ids[1], 0, 0)),
            got,
            got,
            half_spec,
            half_spec,
            pl.BlockSpec((1, 1, rows, width), lambda t, ids: (t, chunk, 0, 0)),
        ],
        pl.BlockSpec((sides, rows, block + LANES), lambda t, ids: (t, 0, 0)),
    )(ids, total, from_down, from_up, late_up, late_down, moment)


def choose(picks, held):
    slots = picks.shape[0] // 2
    _, rows, columns = held[0].shape

    def kernel(picks, *refs):
        sources, out, sem = refs[: len(held)], refs[len(held)], refs[-1]

        @pl.loop(0, slots)
        def _(slot):
            for number, source in enumerate(sources):

                @pl.when(picks[2 * slot] == number)
                def _(source=source):
                    pltpu.make_async_copy(source.at[picks[2 * slot + 1]], out.at[slot], sem).start()

        pltpu.make_async_copy(out, out, sem).wait()

    anywhere = pl.BlockSpec(memory_space=pl.ANY)
    return call(
        kernel,
        jax.ShapeDtypeStruct((slots, rows, columns), BF16),
        (1,),
        [anywhere] * len(held),
        anywhere,
        [pltpu.SemaphoreType.DMA],
    )(picks, *held)


def finish(ids, received, swapped, left_root, right_root, block):
    dp_count, _, rows, _ = received[0].shape
    tile = 256

    def kernel(ids, *refs):
        count = len(received)
        same, other = refs[:count], refs[count : 2 * count]
        left, right, out, grads, shaped = refs[2 * count :]
        core = ids[0]
        power = jnp.zeros((rows, LANES), F32)
        for chunk in range(count):
            for group in range(dp_count):
                for ref, place in ((same[chunk], core), (other[chunk], 1 - core)):
                    at = pl.multiple_of((place * dp_count + group) * (count * rows) + chunk * rows, rows)
                    value = ref[group, 0]
                    grads[pl.ds(at, rows), :] = value[:, :block]
                    power = power + wide(value[:, block:])

        def step(i, total):
            at = pl.ds(pl.multiple_of(i * tile, tile), tile)
            first = jnp.dot(left[0, at, :], grads[...], preferred_element_type=F32).astype(BF16)
            value = jnp.dot(first, right[0], preferred_element_type=F32)
            shaped[at, :] = value
            return total + jnp.sum((value * value).reshape(tile // 8, 8, block), axis=0)

        total = lax.fori_loop(0, block // tile, step, jnp.zeros((8, block), F32))
        scale = jnp.sqrt(jnp.sum(power, keepdims=True)) * lax.rsqrt(jnp.sum(total, keepdims=True) + NORM_EPS)
        owned = ids[1] > 0

        @pl.when(owned)
        def _():
            out[0] = (shaped[...] * scale).astype(BF16)

        @pl.when(jnp.logical_not(owned))
        def _():
            out[0] = jnp.zeros((block, block), BF16)

    def whole(shape):
        return pl.BlockSpec(shape, lambda t, ids: (0,) * len(shape))

    return call(
        kernel,
        jax.ShapeDtypeStruct((1, block, block), BF16),
        (1,),
        [pl.BlockSpec((dp_count, 1) + v.shape[2:], lambda t, ids: (0, 0, 0, 0)) for v in received]
        + [whole(v.shape) for v in swapped]
        + [whole((1, block, block))] * 2,
        whole((1, block, block)),
        [pltpu.VMEM((block, block), BF16), pltpu.VMEM((block, block), F32)],
        cost=1 << 22,
    )(ids, *received, *swapped, left_root, right_root)


def slot_blocks(block_owner, slot_count):
    numbers = jnp.arange(block_owner.shape[0], dtype=jnp.int32)
    queries = jnp.arange(slot_count, dtype=jnp.int32)
    matches = (queries[:, None] == block_owner[None, :]).astype(jnp.int32)
    return jnp.sum(matches * numbers[None, :], axis=1), jnp.sum(matches, axis=1)


def shards(grad_parts, moment, left_roots, right_roots, block_owner):
    dp_count = lax.axis_size("dp")
    mp_count = lax.axis_size("mp")
    dp_index = lax.axis_index("dp")
    mp_index = lax.axis_index("mp")
    matrices = grad_parts.shape[1]
    width = grad_parts.shape[3]
    block = left_roots.shape[1]
    sides = width // block
    rows = moment.shape[1] // CHUNKS
    x, y = dp_index // SIDE, dp_index % SIDE
    z, core = mp_index // 2, mp_index % 2
    ids = jnp.stack([jnp.where(core == 0, x, y), jnp.where(core == 0, y, x), core]).astype(jnp.int32)
    parts = grad_parts.reshape(matrices, dp_count, CHUNKS, rows, width)
    known = moment.reshape(matrices, CHUNKS, rows, width)

    block_of, present = slot_blocks(block_owner, dp_count * mp_count)
    of_plane = lax.dynamic_slice_in_dim(block_of.reshape(dp_count, SIDE, 2), z, 1, 1)[:, 0]
    of_plane = jnp.where(core == 0, of_plane, of_plane[:, ::-1]).reshape(-1)
    offset = (of_plane // sides - z) % SIDE
    column = of_plane // (sides * sides) * sides + of_plane % sides
    picks = jnp.stack([offset, column], axis=1).reshape(-1).astype(jnp.int32)
    own = jnp.stack([core, present[dp_index * mp_count + mp_index]]).astype(jnp.int32)

    received, swapped = [], []
    for chunk in range(CHUNKS):
        up, down = extract(ids, parts, chunk)
        from_down, from_up = send(up, in_plane(0, 1)), send(down, in_plane(0, -1))
        up, down = relay(ids, parts, from_up, from_down, chunk)
        late_down, late_up = send(up, in_plane(0, 1)), send(down, in_plane(0, -1))
        total, up, down = first_sum(ids, parts, from_up, from_down, late_up, late_down, chunk)
        from_down, from_up = send(up, in_plane(1, 1)), send(down, in_plane(1, -1))
        up, down = second_relay(ids, total, from_up, from_down)
        late_down, late_up = send(up, in_plane(1, 1)), send(down, in_plane(1, -1))
        pieces = second_sum(ids, total, from_up, from_down, late_up, late_down, known, chunk, block)
        held = [pieces] + [send(pieces, lambda core, k=k: (0, 0, -k, 0)) for k in (1, 2, 3)]
        outgoing = choose(picks, held).reshape(dp_count, 2, rows, block + LANES)
        arrived = lax.all_to_all(outgoing, "dp", 0, 0, tiled=True)
        received.append(arrived)
        swapped.append(send(arrived[:, 1:], lambda core: (0, 0, 0, 1)))
    return finish(own, received, swapped, left_roots, right_roots, block)


def solution(mesh):
    placed = (
        P("dp", None, "mp", None),
        P(None, ("mp", "dp"), None),
        P(("dp", "mp"), None, None),
        P(("dp", "mp"), None, None),
        P(),
    )
    return jax.shard_map(
        shards, mesh=mesh, in_specs=placed, out_specs=P(("dp", "mp"), None, None), check_vma=False
    )
```

```python
import functools

import jax
import jax.numpy as jnp
from jax import lax
from jax.experimental import pallas as pl
from jax.experimental.pallas import tpu as pltpu
from jax.sharding import PartitionSpec as P

BETA_TWO = 0.999
ADAM_EPS = 1e-08
NORM_EPS = 1e-06
SIDE = 4
CHUNKS = 2
LANES = 128
VMEM_LIMIT = 48 * 1024 * 1024
F32 = jnp.float32
BF16 = jnp.bfloat16


def device_number(x, y, z, core):
    return ((x * SIDE + y) * SIDE + z) * 2 + core


def routes(move):
    pairs = []
    for x in range(SIDE):
        for y in range(SIDE):
            for z in range(SIDE):
                for core in range(2):
                    dx, dy, dz, swap = move(core)
                    target = device_number((x + dx) % SIDE, (y + dy) % SIDE, (z + dz) % SIDE, core ^ swap)
                    pairs.append((device_number(x, y, z, core), target))
    return pairs


def send(value, move):
    return lax.ppermute(value, ("dp", "mp"), routes(move))


def in_plane(phase, sign):
    return lambda core: (sign, 0, 0, 0) if core == phase else (0, sign, 0, 0)


def wide(value):
    return value.astype(F32)


def call(kernel, out_shape, grid, in_specs, out_specs, scratch=(), cost=1, after=()):
    inputs = len(in_specs)
    in_specs = list(in_specs) + [pl.BlockSpec(memory_space=pl.ANY)] * len(after)

    def body(ids, *refs):
        kernel(ids, *refs[:inputs], *refs[len(in_specs) :])

    made = pl.pallas_call(
        body,
        out_shape=out_shape,
        grid_spec=pltpu.PrefetchScalarGridSpec(
            num_scalar_prefetch=1, grid=grid, in_specs=in_specs, out_specs=out_specs, scratch_shapes=list(scratch)
        ),
        compiler_params=pltpu.CompilerParams(vmem_limit_bytes=VMEM_LIMIT),
        cost_estimate=pl.CostEstimate(flops=cost, bytes_accessed=4 * cost, transcendentals=0),
    )
    return lambda *operands: made(*operands, *after)


def row_block(ids, j, q):
    j, q = lax.rem(j + 2 * SIDE, SIDE), lax.rem(q + 2 * SIDE, SIDE)
    return jnp.where(ids[2] == 0, j * SIDE + q, q * SIDE + j)


def grads_spec(m, rows, half, chunk, offset, column, ahead=0):
    def index(t, ids):
        q = t if not ahead else lax.rem(ids[1] + ahead + t, SIDE)
        return 0, row_block(ids, ids[0] + offset, q), chunk, 0, column

    return pl.BlockSpec((m, 1, 1, rows, half), index)


def extract(ids, parts, chunk, pieces, after):
    m, _, _, rows, width = parts.shape
    half = width // 2
    count = len(pieces) // 2

    def kernel(ids, *refs):
        sources, (up, down) = refs[: 2 * count], refs[2 * count :]
        for k in range(count):
            up[k, :, 0] = sources[k][:, 0, 0]
            down[k, :, 0] = sources[count + k][:, 0, 0]

    out = jax.ShapeDtypeStruct((count, m, SIDE, rows, half), BF16)
    out_spec = pl.BlockSpec((count, m, 1, rows, half), lambda t, ids: (0, 0, t, 0, 0))
    return call(
        kernel,
        [out, out],
        (SIDE,),
        [grads_spec(m, rows, half, chunk, *piece) for piece in pieces],
        [out_spec, out_spec],
        after=after,
    )(ids, *([parts] * len(pieces)))


def relay(ids, parts, from_up, from_down, chunk, after):
    m, _, _, rows, width = parts.shape
    half = width // 2

    def kernel(ids, a, b, below, above, up, down):
        up[:, 0] = (wide(a[:, 0, 0]) + wide(below[0, :, 0])).astype(BF16)
        down[:, 0] = (wide(b[:, 0, 0]) + wide(above[0, :, 0])).astype(BF16)

    spec = functools.partial(grads_spec, m, rows, half, chunk)
    out = jax.ShapeDtypeStruct((m, SIDE, rows, half), BF16)
    out_spec = pl.BlockSpec((m, 1, rows, half), lambda t, ids: (0, t, 0, 0))
    got = pl.BlockSpec((1, m, 1, rows, half), lambda t, ids: (0, 0, t, 0, 0))
    return call(
        kernel, [out, out], (SIDE,), [spec(1, 1), spec(-1, 0), got, got], [out_spec, out_spec], after=after
    )(ids, parts, parts, from_down, from_up)


def first_sum(ids, parts, from_up, from_down, late_up, late_down, chunk, after):
    m, _, _, rows, width = parts.shape
    half = width // 2

    def kernel(ids, own, below, above, late_above, late_below, mine, *others):
        t = pl.program_id(0)
        left = (wide(own[:, 0, 0, :, :half]) + wide(below[0, :, 0]) + wide(late_above[:, 0])).astype(BF16)
        right = (wide(own[:, 0, 0, :, half:]) + wide(above[0, :, 0]) + wide(late_below[:, 0])).astype(BF16)
        for number, out in enumerate((*others, mine)):

            @pl.when(t == number)
            def _(out=out):
                out[:, :, :half] = left
                out[:, :, half:] = right

    def at(t, ids):
        return lax.rem(ids[1] + 1 + t, SIDE)

    raw = from_up.shape[0] - 1
    got = pl.BlockSpec((1, m, 1, rows, half), lambda t, ids: (raw, 0, at(t, ids), 0, 0))
    late = pl.BlockSpec((m, 1, rows, half), lambda t, ids: (0, at(t, ids), 0, 0))
    whole = pl.BlockSpec((m, rows, width), lambda t, ids: (0, 0, 0))
    return call(
        kernel,
        [jax.ShapeDtypeStruct((m, rows, width), BF16)] * SIDE,
        (SIDE,),
        [grads_spec(m, rows, width, chunk, 0, 0, ahead=1), got, got, late, late],
        [whole] * SIDE,
        after=after,
    )(ids, parts, from_down, from_up, late_up, late_down)


def second_sum(ids, sums, moment, chunk, block, earlier, after):
    m, rows, width = sums[0].shape
    sides = width // block
    last = len(earlier) > 0

    def kernel(ids, *refs):
        terms, known, out = refs[: len(sums)], refs[len(sums)], refs[len(sums) + 1 + len(earlier)]
        for side in range(sides):
            at = side * block
            power = refs[len(sums) + 1][side] if last else jnp.zeros((rows, LANES), F32)
            for k in range(at, at + block, LANES):
                gradient = sum(wide(term[0, :, k : k + LANES]) for term in terms)
                second = BETA_TWO * known[0, 0, :, k : k + LANES] + (1.0 - BETA_TWO) * gradient * gradient
                direction = gradient / (jnp.sqrt(second) + ADAM_EPS)
                power = power + direction * direction
                out[side, :, k - at : k - at + LANES] = gradient.astype(BF16)
            if last:
                out[side, :, block:] = power.astype(BF16)
            else:
                refs[-1][side] = power

    power_spec = pl.BlockSpec((sides, rows, LANES), lambda t, ids: (t, 0, 0))
    columns = block + LANES * last
    shapes = [jax.ShapeDtypeStruct((m * sides, rows, columns), BF16)]
    specs = [pl.BlockSpec((sides, rows, columns), lambda t, ids: (t, 0, 0))]
    if not last:
        shapes.append(jax.ShapeDtypeStruct((m * sides, rows, LANES), F32))
        specs.append(power_spec)
    return call(
        kernel,
        shapes,
        (m,),
        [pl.BlockSpec((1, rows, width), lambda t, ids: (t, 0, 0))] * len(sums)
        + [pl.BlockSpec((1, 1, rows, width), lambda t, ids: (t, chunk, 0, 0))]
        + [power_spec] * len(earlier),
        specs,
        after=after,
    )(ids, *sums, moment, *earlier)


def choose(picks, held, columns, after):
    slots = picks.shape[0] // 2
    count = len(held[0])
    rows = held[0][0].shape[1]

    def kernel(picks, *refs):
        sources, out, sem = refs[: 2 * count], refs[2 * count], refs[-1]

        @pl.loop(0, slots)
        def _(slot):
            for number in range(count):

                @pl.when(picks[2 * slot] == number)
                def _(number=number):
                    for chunk in range(2):
                        piece = sources[chunk * count + number].at[picks[2 * slot + 1]]
                        there = out.at[slot, chunk, :, pl.ds(0, piece.shape[1])]
                        pltpu.make_async_copy(piece, there, sem).start()

        for chunk in range(2):
            there = out.at[:, chunk, :, pl.ds(0, sources[chunk * count].shape[2])]
            pltpu.make_async_copy(there, there, sem).wait()

    anywhere = pl.BlockSpec(memory_space=pl.ANY)
    return call(
        kernel,
        jax.ShapeDtypeStruct((slots, 2, rows, columns), BF16),
        (1,),
        [anywhere] * (2 * count),
        pl.BlockSpec((slots, 2, rows, columns), lambda t, ids: (0, 0, 0, 0)),
        [pltpu.SemaphoreType.DMA],
        after=after,
    )(picks, *held[0], *held[1])


def finish(ids, same, other, left_root, right_root, block):
    dp_count, _, _, rows, _ = same.shape
    tile = 512

    def kernel(ids, same, other, left, right, out, grads, powers, shaped, sem):
        core = ids[0]
        copies = []
        for k, (ref, place) in enumerate(((same, core), (other, 1 - core))):
            source = ref.at[:, k]
            copies.append(pltpu.make_async_copy(source.at[:, :, :, pl.ds(0, block)], grads.at[place], sem.at[0]))
            copies.append(pltpu.make_async_copy(source.at[:, 1, :, pl.ds(block, LANES)], powers.at[k], sem.at[1]))
        for copy in copies:
            copy.start()
        pltpu.make_async_copy(grads, grads, sem.at[0]).wait()

        def step(i, total):
            at = pl.ds(pl.multiple_of(i * tile, tile), tile)
            whole = grads[...].reshape(block, block)
            first = jnp.dot(left[0, at, :], whole, preferred_element_type=F32).astype(BF16)
            value = jnp.dot(first, right[0], preferred_element_type=F32)
            shaped[at, :] = value
            return total + jnp.sum((value * value).reshape(tile // 8, 8, block), axis=0)

        total = lax.fori_loop(0, block // tile, step, jnp.zeros((8, block), F32))
        pltpu.make_async_copy(powers, powers, sem.at[1]).wait()
        power = jnp.sum(wide(powers[...]).reshape(-1, 8, LANES), axis=0)
        scale = jnp.sqrt(jnp.sum(power, keepdims=True)) * lax.rsqrt(jnp.sum(total, keepdims=True) + NORM_EPS)
        owned = ids[1] > 0

        @pl.when(owned)
        def _():
            out[0] = (shaped[...] * scale).astype(BF16)

        @pl.when(jnp.logical_not(owned))
        def _():
            out[0] = jnp.zeros((block, block), BF16)

    root = pl.BlockSpec((1, block, block), lambda t, ids: (0, 0, 0))
    return call(
        kernel,
        jax.ShapeDtypeStruct((1, block, block), BF16),
        (1,),
        [pl.BlockSpec(memory_space=pl.ANY)] * 2 + [root, root],
        root,
        [
            pltpu.VMEM((2, dp_count, 2, rows, block), BF16),
            pltpu.VMEM((2, dp_count, rows, LANES), BF16),
            pltpu.VMEM((block, block), F32),
            pltpu.SemaphoreType.DMA((2,)),
        ],
        cost=1 << 20,
    )(ids, same, other, left_root, right_root)


def slot_blocks(block_owner, slot_count):
    numbers = jnp.arange(block_owner.shape[0], dtype=jnp.int32)
    queries = jnp.arange(slot_count, dtype=jnp.int32)
    matches = (queries[:, None] == block_owner[None, :]).astype(jnp.int32)
    return jnp.sum(matches * numbers[None, :], axis=1), jnp.sum(matches, axis=1)


def shards(grad_parts, moment, left_roots, right_roots, block_owner):
    dp_count = lax.axis_size("dp")
    mp_count = lax.axis_size("mp")
    dp_index = lax.axis_index("dp")
    mp_index = lax.axis_index("mp")
    matrices = grad_parts.shape[1]
    width = grad_parts.shape[3]
    block = left_roots.shape[1]
    sides = width // block
    rows = moment.shape[1] // CHUNKS
    x, y = dp_index // SIDE, dp_index % SIDE
    z, core = mp_index // 2, mp_index % 2
    ids = jnp.stack([jnp.where(core == 0, x, y), jnp.where(core == 0, y, x), core]).astype(jnp.int32)
    parts = grad_parts.reshape(matrices, dp_count, CHUNKS, rows, width)
    known = moment.reshape(matrices, CHUNKS, rows, width)

    block_of, present = slot_blocks(block_owner, dp_count * mp_count)
    of_plane = lax.dynamic_slice_in_dim(block_of.reshape(dp_count, SIDE, 2), z, 1, 1)[:, 0]
    of_plane = jnp.where(core == 0, of_plane, of_plane[:, ::-1])
    column = of_plane // (sides * sides) * sides + of_plane % sides
    plane = of_plane // sides % SIDE
    picks = jnp.stack([(plane - z) % SIDE, column], axis=2).reshape(-1)
    own = jnp.stack([core, present[dp_index * mp_count + mp_index]])

    def along(phase, up, down):
        return send(down, in_plane(phase, -1)), send(up, in_plane(phase, 1))

    def second_axis(mine, up, far, down):
        return [mine, send(far, in_plane(1, 2)), send(up, in_plane(1, 1)), send(down, in_plane(1, -1))]

    last = ()
    sent, late, sums = [], [], []
    for chunk in range(CHUNKS):
        up, down = extract(ids, parts, chunk, ((2, 1), (1, 0), (-2, 0), (-1, 1)), last)
        last = (up,)
        sent.append(along(0, up, down))
    for chunk in range(CHUNKS):
        up, down = relay(ids, parts, *sent[chunk], chunk, last)
        last = (up,)
        late.append(along(0, up, down))
    for chunk in range(CHUNKS):
        terms = first_sum(ids, parts, *sent[chunk], *late[chunk], chunk, last)
        last = (terms[0],)
        sums.append(second_axis(*terms))
    held = []
    power = []
    for chunk in range(CHUNKS):
        pieces, *power = second_sum(ids, sums[chunk], known, chunk, block, power, last)
        last = (pieces,)
        held.append([pieces] + [send(pieces, lambda core, k=k: (0, 0, -k, 0)) for k in (1, 2, 3)])
    outgoing = choose(picks, held, block + LANES, last)
    outgoing = outgoing.reshape(dp_count, 2, CHUNKS, rows, block + LANES)
    same = lax.all_to_all(outgoing, "dp", 0, 0, tiled=True)
    other = send(same, lambda core: (0, 0, 0, 1))
    return finish(own, same, other, left_roots, right_roots, block)


def solution(mesh):
    placed = (
        P("dp", None, "mp", None),
        P(None, ("mp", "dp"), None),
        P(("dp", "mp"), None, None),
        P(("dp", "mp"), None, None),
        P(),
    )
    return jax.shard_map(
        shards, mesh=mesh, in_specs=placed, out_specs=P(("dp", "mp"), None, None), check_vma=False
    )
```

```python
import functools

import jax
import jax.numpy as jnp
from jax import lax
from jax.experimental import pallas as pl
from jax.experimental.pallas import tpu as pltpu
from jax.sharding import PartitionSpec as P

BETA_TWO = 0.999
ADAM_EPS = 1e-08
NORM_EPS = 1e-06
SIDE = 4
CHUNKS = 2
LANES = 128
PIECES = 12
VMEM_LIMIT = 12 * 1024 * 1024
VMEM_MOST = 48 * 1024 * 1024
F32 = jnp.float32
BF16 = jnp.bfloat16


def device_number(x, y, z, core):
    return ((x * SIDE + y) * SIDE + z) * 2 + core


def routes(move):
    pairs = []
    for x in range(SIDE):
        for y in range(SIDE):
            for z in range(SIDE):
                for core in range(2):
                    dx, dy, dz, swap = move(core)
                    target = device_number((x + dx) % SIDE, (y + dy) % SIDE, (z + dz) % SIDE, core ^ swap)
                    pairs.append((device_number(x, y, z, core), target))
    return pairs


def send(value, move):
    return lax.ppermute(value, ("dp", "z", "core"), routes(move))


def in_plane(phase, sign):
    return lambda core: (sign, 0, 0, 0) if core == phase else (0, sign, 0, 0)


def wide(value):
    return value.astype(F32)


def call(kernel, out_shape, grid, in_specs, out_specs, scratch=(), cost=1, after=(), grant=VMEM_MOST):
    inputs = len(in_specs)
    in_specs = list(in_specs) + [pl.BlockSpec(memory_space=pl.ANY)] * len(after)

    def body(ids, *refs):
        kernel(ids, *refs[:inputs], *refs[len(in_specs) :])

    made = pl.pallas_call(
        body,
        out_shape=out_shape,
        grid_spec=pltpu.PrefetchScalarGridSpec(
            num_scalar_prefetch=1, grid=grid, in_specs=in_specs, out_specs=out_specs, scratch_shapes=list(scratch)
        ),
        compiler_params=pltpu.CompilerParams(vmem_limit_bytes=grant),
        cost_estimate=pl.CostEstimate(flops=cost, bytes_accessed=4 * cost, transcendentals=0),
    )
    return lambda *operands: made(*operands, *after)


def row_block(ids, j, q):
    j, q = lax.rem(j + 2 * SIDE, SIDE), lax.rem(q + 2 * SIDE, SIDE)
    return jnp.where(ids[2] == 0, j * SIDE + q, q * SIDE + j)


def grads_spec(m, rows, half, chunk, offset, column, ahead=0):
    def index(t, ids):
        q = t if not ahead else lax.rem(ids[1] + ahead + t, SIDE)
        return 0, row_block(ids, ids[0] + offset, q), chunk, 0, column

    return pl.BlockSpec((m, 1, 1, rows, half), index)


def extract(ids, parts, chunk, pieces, after):
    m, _, _, rows, width = parts.shape
    half = width // 2
    count = len(pieces) // 2

    def kernel(ids, *refs):
        sources, (up, down) = refs[: 2 * count], refs[2 * count :]
        for k in range(count):
            up[k, :, 0] = sources[k][:, 0, 0]
            down[k, :, 0] = sources[count + k][:, 0, 0]

    out = jax.ShapeDtypeStruct((count, m, SIDE, rows, half), BF16)
    out_spec = pl.BlockSpec((count, m, 1, rows, half), lambda t, ids: (0, 0, t, 0, 0))
    return call(
        kernel,
        [out, out],
        (SIDE,),
        [grads_spec(m, rows, half, chunk, *piece) for piece in pieces],
        [out_spec, out_spec],
        after=after,
    )(ids, *([parts] * len(pieces)))


def relay(ids, parts, from_up, from_down, chunk, after):
    m, _, _, rows, width = parts.shape
    half = width // 2

    def kernel(ids, a, b, below, above, up, down):
        up[:, 0] = (wide(a[:, 0, 0]) + wide(below[0, :, 0])).astype(BF16)
        down[:, 0] = (wide(b[:, 0, 0]) + wide(above[0, :, 0])).astype(BF16)

    spec = functools.partial(grads_spec, m, rows, half, chunk)
    out = jax.ShapeDtypeStruct((m, SIDE, rows, half), BF16)
    out_spec = pl.BlockSpec((m, 1, rows, half), lambda t, ids: (0, t, 0, 0))
    got = pl.BlockSpec((1, m, 1, rows, half), lambda t, ids: (0, 0, t, 0, 0))
    return call(
        kernel, [out, out], (SIDE,), [spec(1, 1), spec(-1, 0), got, got], [out_spec, out_spec], after=after
    )(ids, parts, parts, from_down, from_up)


def first_sum(ids, parts, from_up, from_down, late_up, late_down, chunk, after):
    m, _, _, rows, width = parts.shape
    half = width // 2

    def kernel(ids, own, below, above, late_above, late_below, mine, *others):
        t = pl.program_id(0)
        left = (wide(own[:, 0, 0, :, :half]) + wide(below[0, :, 0]) + wide(late_above[:, 0])).astype(BF16)
        right = (wide(own[:, 0, 0, :, half:]) + wide(above[0, :, 0]) + wide(late_below[:, 0])).astype(BF16)
        for number, out in enumerate((*others, mine)):

            @pl.when(t == number)
            def _(out=out):
                out[:, :, :half] = left
                out[:, :, half:] = right

    def at(t, ids):
        return lax.rem(ids[1] + 1 + t, SIDE)

    raw = from_up.shape[0] - 1
    got = pl.BlockSpec((1, m, 1, rows, half), lambda t, ids: (raw, 0, at(t, ids), 0, 0))
    late = pl.BlockSpec((m, 1, rows, half), lambda t, ids: (0, at(t, ids), 0, 0))
    whole = pl.BlockSpec((m, rows, width), lambda t, ids: (0, 0, 0))
    return call(
        kernel,
        [jax.ShapeDtypeStruct((m, rows, width), BF16)] * SIDE,
        (SIDE,),
        [grads_spec(m, rows, width, chunk, 0, 0, ahead=1), got, got, late, late],
        [whole] * SIDE,
        after=after,
    )(ids, parts, from_down, from_up, late_up, late_down)


def second_sum(ids, sums, moment, chunk, block, earlier, after):
    m, rows, width = sums[0].shape
    sides = width // block
    tiles = block // LANES
    last = len(earlier) > 0

    def kernel(ids, *refs):
        terms, known = refs[: len(sums)], refs[len(sums)]
        t = pl.program_id(0)
        if last:
            before, out, powers = refs[len(sums) + 1 :]
        else:
            out, powers = refs[len(sums) + 1 :]
        for side in range(sides):
            power = before[side] if last else jnp.zeros((rows, LANES), F32)
            for tile in range(tiles):
                at = pl.ds(side * block + tile * LANES, LANES)
                gradient = sum(wide(term[0, :, at]) for term in terms)
                second = BETA_TWO * known[0, 0, :, at] + (1.0 - BETA_TWO) * gradient * gradient
                direction = gradient / (jnp.sqrt(second) + ADAM_EPS)
                power = power + direction * direction
                out[(t * sides + side) * tiles + tile] = gradient.astype(BF16)
            if last:
                row = lax.broadcasted_iota(jnp.int32, (rows, LANES), 0)
                placed = jnp.where(row == t * sides + side, jnp.sum(power, axis=0, keepdims=True), 0.0)
                powers[...] = jnp.where(t + side == 0, 0.0, powers[...]) + placed
            else:
                powers[side] = power
        if last:

            @pl.when(t == m - 1)
            def _():
                out[m * sides * tiles] = powers[...].astype(BF16)

    power_spec = pl.BlockSpec((sides, rows, LANES), lambda t, ids: (t, 0, 0))
    shapes = [jax.ShapeDtypeStruct((m * sides * tiles + last, rows, LANES), BF16)]
    specs = [pl.BlockSpec((m * sides * tiles + last, rows, LANES), lambda t, ids: (0, 0, 0))]
    if not last:
        shapes.append(jax.ShapeDtypeStruct((m * sides, rows, LANES), F32))
        specs.append(power_spec)
    return call(
        kernel,
        shapes,
        (m,),
        [pl.BlockSpec((1, rows, width), lambda t, ids: (t, 0, 0))] * len(sums)
        + [pl.BlockSpec((1, 1, rows, width), lambda t, ids: (t, chunk, 0, 0))]
        + [power_spec] * len(earlier),
        specs,
        [pltpu.VMEM((rows, LANES), F32)] * last,
        after=after,
        grant=VMEM_LIMIT,
    )(ids, *sums, moment, *earlier)


def choose(picks, held, after):
    slots = picks.shape[0] // 2
    count = len(held[0])
    total, rows, _ = held[0][0].shape
    tiles = total // PIECES

    def kernel(picks, *refs):
        first, second, out = refs[:count], refs[count : 2 * count], refs[2 * count]

        @pl.loop(0, slots)
        def _(slot):
            piece = pl.ds(picks[2 * slot + 1] * tiles, tiles)
            for number in range(count):

                @pl.when(picks[2 * slot] == number)
                def _(number=number):
                    out[slot, :tiles] = first[number][piece]
                    out[slot, tiles : 2 * tiles] = second[number][piece]
                    out[slot, 2 * tiles] = second[number][total]

    def whole(shape):
        return pl.BlockSpec(shape, lambda t, ids: (0,) * len(shape))

    shape = (slots, 2 * tiles + 1, rows, LANES)
    return call(
        kernel,
        jax.ShapeDtypeStruct(shape, BF16),
        (1,),
        [whole(v.shape) for v in (*held[0], *held[1])],
        whole(shape),
        after=after,
        grant=VMEM_LIMIT,
    )(picks, *held[0], *held[1])


def finish(ids, received, left_root, right_root, block):
    dp_count, _, _, rows, _ = received.shape
    tiles = block // LANES
    step = block // 2

    def kernel(ids, received, left, right, out, landed, grads, lefts, rights, shaped, results, sem):
        get = pltpu.make_async_copy(received, landed, sem.at[0])
        get_left = pltpu.make_async_copy(left.at[0], lefts, sem.at[1])
        get_right = pltpu.make_async_copy(right.at[0], rights, sem.at[2])
        get.start()
        get_left.start()
        get_right.start()
        get.wait()

        @pl.loop(0, dp_count)
        def _(group):
            for core in range(2):
                for tile in range(2 * tiles):
                    columns = slice(tile % tiles * LANES, (tile % tiles + 1) * LANES)
                    grads[core, group, tile // tiles, :, columns] = landed[group, core, tile]

        get_left.wait()
        total = jnp.zeros((8, block), F32)
        for at in range(0, block, step):
            whole = grads[...].reshape(block, block)
            first = jnp.dot(lefts[at : at + step, :], whole, preferred_element_type=F32).astype(BF16)
            if at == 0:
                get_right.wait()
            value = jnp.dot(first, rights[...], preferred_element_type=F32)
            shaped[at : at + step, :] = value
            total = total + jnp.sum((value * value).reshape(step // 8, 8, block), axis=0)
        powers = wide(landed[:, :, 2 * tiles])
        row = lax.broadcasted_iota(jnp.int32, powers.shape, 2)
        power = jnp.sum(jnp.where(row == ids[1], powers, 0.0).reshape(-1, 8, LANES), axis=0)
        scale = jnp.sqrt(jnp.sum(power, keepdims=True)) * lax.rsqrt(jnp.sum(total, keepdims=True) + NORM_EPS)
        owned = ids[0] > 0
        for at in range(0, block, step):
            here = pl.ds(at, step)

            @pl.when(owned)
            def _():
                results[here] = (shaped[here] * scale).astype(BF16)

            @pl.when(jnp.logical_not(owned))
            def _():
                results[here] = jnp.zeros((step, block), BF16)

            pltpu.make_async_copy(results.at[here], out.at[0, here], sem.at[3]).start()
        pltpu.make_async_copy(results, out.at[0], sem.at[3]).wait()

    anywhere = pl.BlockSpec(memory_space=pl.ANY)
    return call(
        kernel,
        jax.ShapeDtypeStruct((1, block, block), BF16),
        (1,),
        [anywhere] * 3,
        anywhere,
        [
            pltpu.VMEM(received.shape, BF16),
            pltpu.VMEM((2, dp_count, 2, rows, block), BF16),
            pltpu.VMEM((block, block), BF16),
            pltpu.VMEM((block, block), BF16),
            pltpu.VMEM((block, block), F32),
            pltpu.VMEM((block, block), BF16),
            pltpu.SemaphoreType.DMA((4,)),
        ],
        cost=1 << 20,
        grant=60 * 1024 * 1024,
    )(ids, received, left_root, right_root)


def slot_blocks(block_owner, slot_count):
    numbers = jnp.arange(block_owner.shape[0], dtype=jnp.int32)
    queries = jnp.arange(slot_count, dtype=jnp.int32)
    matches = (queries[:, None] == block_owner[None, :]).astype(jnp.int32)
    return jnp.sum(matches * numbers[None, :], axis=1), jnp.sum(matches, axis=1)


def shards(grad_parts, moment, left_roots, right_roots, block_owner):
    dp_count = lax.axis_size("dp")
    dp_index = lax.axis_index("dp")
    matrices = grad_parts.shape[1]
    width = grad_parts.shape[3]
    block = left_roots.shape[1]
    sides = width // block
    rows = moment.shape[1] // CHUNKS
    x, y = dp_index // SIDE, dp_index % SIDE
    z, core = lax.axis_index("z"), lax.axis_index("core")
    ids = jnp.stack([jnp.where(core == 0, x, y), jnp.where(core == 0, y, x), core]).astype(jnp.int32)
    parts = grad_parts.reshape(matrices, dp_count, CHUNKS, rows, width)
    known = moment.reshape(matrices, CHUNKS, rows, width)

    block_of, present = slot_blocks(block_owner, dp_count * SIDE * 2)
    of_plane = lax.dynamic_slice_in_dim(block_of.reshape(dp_count, SIDE, 2), z, 1, 1).reshape(-1)
    column = of_plane // (sides * sides) * sides + of_plane % sides
    plane = of_plane // sides % SIDE
    picks = jnp.stack([(plane - z) % SIDE, column], axis=1).reshape(-1)
    mine = device_number(x, y, z, core)
    own_block = block_of[mine]
    own = jnp.stack([present[mine], own_block // (sides * sides) * sides + own_block % sides])

    def along(phase, up, down):
        return send(down, in_plane(phase, -1)), send(up, in_plane(phase, 1))

    def second_axis(mine, up, far, down):
        return [mine, send(down, in_plane(1, -1)), send(up, in_plane(1, 1)), send(far, in_plane(1, 2))]

    last = ()
    sent, late, sums = [], [], []
    for chunk in range(CHUNKS):
        up, down = extract(ids, parts, chunk, ((2, 1), (1, 0), (-2, 0), (-1, 1)), last)
        last = (up,)
        sent.append(along(0, up, down))
    for chunk in range(CHUNKS):
        up, down = relay(ids, parts, *sent[chunk], chunk, last)
        last = (up,)
        late.append(along(0, up, down))
    for chunk in range(CHUNKS):
        terms = first_sum(ids, parts, *sent[chunk], *late[chunk], chunk, last)
        last = (terms[0],)
        sums.append(second_axis(*terms))
    held = []
    power = []
    for chunk in range(CHUNKS):
        pieces, *power = second_sum(ids, sums[chunk], known, chunk, block, power, last)
        last = (pieces,)
        held.append([pieces] + [send(pieces, lambda core, k=k: (0, 0, -k, 0)) for k in (1, 2, 3)])
    outgoing = choose(picks, held, last)
    received = lax.all_to_all(outgoing, ("dp", "core"), 0, 0, tiled=True)
    received = received.reshape((dp_count, 2) + received.shape[1:])
    return finish(own, received, left_roots, right_roots, block)


def solution(mesh):
    split = jax.sharding.Mesh(mesh.devices.reshape(-1, SIDE, 2), ("dp", "z", "core"))
    placed = (
        P("dp", None, ("z", "core"), None),
        P(None, ("z", "core", "dp"), None),
        P(("dp", "z", "core"), None, None),
        P(("dp", "z", "core"), None, None),
        P(),
    )
    return jax.shard_map(
        shards, mesh=split, in_specs=placed, out_specs=P(("dp", "z", "core"), None, None), check_vma=False
    )
```

```python
import jax
import jax.numpy as jnp
from jax import lax
from jax.experimental import pallas as pl
from jax.experimental.pallas import tpu as pltpu
from jax.sharding import PartitionSpec as P

BETA_TWO = 0.999
ADAM_EPS = 1e-08
NORM_EPS = 1e-06
SIDE = 4
CHUNKS = 2
LANES = 128
PIECES = 12
VMEM_LIMIT = 12 * 1024 * 1024
VMEM_MOST = 20 * 1024 * 1024
F32 = jnp.float32
BF16 = jnp.bfloat16


def device_number(x, y, z, core):
    return ((x * SIDE + y) * SIDE + z) * 2 + core


def routes(move):
    pairs = []
    for x in range(SIDE):
        for y in range(SIDE):
            for z in range(SIDE):
                for core in range(2):
                    dx, dy, dz, swap = move(core)
                    target = device_number((x + dx) % SIDE, (y + dy) % SIDE, (z + dz) % SIDE, core ^ swap)
                    pairs.append((device_number(x, y, z, core), target))
    return pairs


def send(value, move):
    return lax.ppermute(value, ("dp", "z", "core"), routes(move))


def in_plane(phase, sign):
    return lambda core: (sign, 0, 0, 0) if core == phase else (0, sign, 0, 0)


def wide(value):
    return value.astype(F32)


def in_vmem(value):
    return pltpu.with_memory_space_constraint(value, pltpu.VMEM)


def call(kernel, out_shape, grid, in_specs, out_specs, scratch=(), cost=1, after=(), grant=VMEM_MOST):
    inputs = len(in_specs)
    in_specs = list(in_specs) + [pl.BlockSpec(memory_space=pl.ANY)] * len(after)

    def body(ids, *refs):
        kernel(ids, *refs[:inputs], *refs[len(in_specs) :])

    made = pl.pallas_call(
        body,
        out_shape=out_shape,
        grid_spec=pltpu.PrefetchScalarGridSpec(
            num_scalar_prefetch=1, grid=grid, in_specs=in_specs, out_specs=out_specs, scratch_shapes=list(scratch)
        ),
        compiler_params=pltpu.CompilerParams(vmem_limit_bytes=grant),
        cost_estimate=pl.CostEstimate(flops=cost, bytes_accessed=4 * cost, transcendentals=0),
    )
    return lambda *operands: made(*operands, *after)


def row_block(ids, j, q):
    j, q = lax.rem(j + 2 * SIDE, SIDE), lax.rem(q + 2 * SIDE, SIDE)
    return jnp.where(ids[2] == 0, j * SIDE + q, q * SIDE + j)


def extract(ids, parts, chunk, pieces, after):
    m, _, _, rows, width = parts.shape
    half = width // 2
    count = len(pieces) // 2

    def kernel(ids, source, up, down, sem):
        copies = []
        for number, (offset, column) in enumerate(pieces):
            out, part = (up, down)[number // count], number % count
            for q in range(SIDE):
                block = row_block(ids, ids[0] + offset, q)
                place = source.at[:, block, chunk, :, pl.ds(column * half, half)]
                copies.append(pltpu.make_async_copy(place, out.at[part, :, q], sem.at[number, q]))
        for copy in copies:
            copy.start()
        for copy in copies:
            copy.wait()

    here = pl.BlockSpec(memory_space=pltpu.VMEM)
    return call(
        kernel,
        [pltpu.VMEM((count, m, SIDE, rows, half), BF16)] * 2,
        (1,),
        [pl.BlockSpec(memory_space=pl.ANY)],
        [here, here],
        [pltpu.SemaphoreType.DMA((2 * count, SIDE))],
        after=after,
    )(ids, parts)


def relay(ids, own_up, own_down, from_up, from_down, after):
    _, m, _, rows, half = own_up.shape

    def kernel(ids, a, b, below, above, up, down):
        q = pl.program_id(0)
        up[:, q] = (wide(a[0, :, q]) + wide(below[0, :, q])).astype(BF16)
        down[:, q] = (wide(b[0, :, q]) + wide(above[0, :, q])).astype(BF16)

    here = pl.BlockSpec(memory_space=pltpu.VMEM)
    return call(
        kernel,
        [pltpu.VMEM((m, SIDE, rows, half), BF16)] * 2,
        (SIDE,),
        [here] * 4,
        [here, here],
        after=after,
    )(ids, *(in_vmem(value) for value in (own_up, own_down, from_down, from_up)))


def first_sum(ids, own_up, own_down, from_up, from_down, late_up, late_down, after):
    _, m, _, rows, half = own_up.shape

    def kernel(ids, own_left, own_right, below, above, late_above, late_below, mine, *others):
        t = pl.program_id(0)
        q = lax.rem(ids[1] + 1 + t, SIDE)
        left = (wide(own_left[1, :, q]) + wide(below[1, :, q]) + wide(late_above[:, q])).astype(BF16)
        right = (wide(own_right[1, :, q]) + wide(above[1, :, q]) + wide(late_below[:, q])).astype(BF16)
        for number, out in enumerate((*others, mine)):

            @pl.when(t == number)
            def _(out=out):
                out[:, :, :half] = left
                out[:, :, half:] = right

    here = pl.BlockSpec(memory_space=pltpu.VMEM)
    return call(
        kernel,
        [pltpu.VMEM((m, rows, 2 * half), BF16)] * SIDE,
        (SIDE,),
        [here] * 6,
        [here] * SIDE,
        after=after,
    )(ids, *(in_vmem(value) for value in (own_up, own_down, from_down, from_up, late_up, late_down)))


def second_sum(ids, sums, moment, chunk, block, earlier, after):
    m, rows, width = sums[0].shape
    sides = width // block
    tiles = block // LANES
    last = len(earlier) > 0

    def kernel(ids, *refs):
        terms, known = refs[: len(sums)], refs[len(sums)]
        t = pl.program_id(0)
        if last:
            before, out, powers = refs[len(sums) + 1 :]
        else:
            out, powers = refs[len(sums) + 1 :]
        for side in range(sides):
            power = before[side] if last else jnp.zeros((rows, LANES), F32)
            for tile in range(tiles):
                at = pl.ds(side * block + tile * LANES, LANES)
                gradient = sum(wide(term[0, :, at]) for term in terms)
                second = BETA_TWO * known[0, 0, :, at] + (1.0 - BETA_TWO) * gradient * gradient
                direction = gradient / (jnp.sqrt(second) + ADAM_EPS)
                power = power + direction * direction
                out[(t * sides + side) * tiles + tile] = gradient.astype(BF16)
            if last:
                row = lax.broadcasted_iota(jnp.int32, (rows, LANES), 0)
                placed = jnp.where(row == t * sides + side, jnp.sum(power, axis=0, keepdims=True), 0.0)
                powers[...] = jnp.where(t + side == 0, 0.0, powers[...]) + placed
            else:
                powers[side] = power
        if last:

            @pl.when(t == m - 1)
            def _():
                out[m * sides * tiles] = powers[...].astype(BF16)

    power_spec = pl.BlockSpec((sides, rows, LANES), lambda t, ids: (t, 0, 0))
    shapes = [jax.ShapeDtypeStruct((m * sides * tiles + last, rows, LANES), BF16)]
    specs = [pl.BlockSpec((m * sides * tiles + last, rows, LANES), lambda t, ids: (0, 0, 0))]
    if not last:
        shapes.append(jax.ShapeDtypeStruct((m * sides, rows, LANES), F32))
        specs.append(power_spec)
    return call(
        kernel,
        shapes,
        (m,),
        [pl.BlockSpec((1, rows, width), lambda t, ids: (t, 0, 0))] * len(sums)
        + [pl.BlockSpec((1, 1, rows, width), lambda t, ids: (t, chunk, 0, 0))]
        + [power_spec] * len(earlier),
        specs,
        [pltpu.VMEM((rows, LANES), F32)] * last,
        after=after,
        grant=VMEM_LIMIT,
    )(ids, *sums, moment, *earlier)


def choose(picks, held, after):
    slots = picks.shape[0] // 2
    count = len(held[0])
    total, rows, _ = held[0][0].shape
    tiles = total // PIECES
    steps = 4

    def kernel(picks, *refs):
        first, second, out = refs[:count], refs[count : 2 * count], refs[2 * count]

        @pl.loop(0, slots // steps)
        def _(k):
            slot = pl.program_id(0) * (slots // steps) + k
            piece = pl.ds(picks[2 * slot + 1] * tiles, tiles)
            for number in range(count):

                @pl.when(picks[2 * slot] == number)
                def _(number=number):
                    out[k, :tiles] = first[number][piece]
                    out[k, tiles : 2 * tiles] = second[number][piece]
                    out[k, 2 * tiles] = second[number][total]

    shape = (slots, 2 * tiles + 1, rows, LANES)
    return call(
        kernel,
        jax.ShapeDtypeStruct(shape, BF16),
        (steps,),
        [pl.BlockSpec(memory_space=pltpu.VMEM)] * (2 * count),
        pl.BlockSpec((slots // steps,) + shape[1:], lambda t, ids: (t, 0, 0, 0)),
        after=after,
        grant=VMEM_LIMIT,
    )(picks, *(in_vmem(value) for value in (*held[0], *held[1])))


def finish(ids, received, left_root, right_root, block):
    dp_count, _, _, rows, _ = received.shape
    tiles = block // LANES
    step = block // 2

    def kernel(ids, received, left, right, out, grads, lefts, rights, shaped, results, sem):
        get_lefts = [
            pltpu.make_async_copy(left.at[0, pl.ds(at, step)], lefts.at[pl.ds(at, step)], sem.at[at // step])
            for at in range(0, block, step)
        ]
        get_right = pltpu.make_async_copy(right.at[0], rights, sem.at[2])
        get_lefts[0].start()
        get_right.start()
        get_lefts[1].start()

        @pl.loop(0, dp_count)
        def _(group):
            for core in range(2):
                for tile in range(2 * tiles):
                    columns = slice(tile % tiles * LANES, (tile % tiles + 1) * LANES)
                    grads[core, group, tile // tiles, :, columns] = received[group, core, tile]

        total = jnp.zeros((8, block), F32)
        for at in range(0, block, step):
            whole = grads[...].reshape(block, block)
            get_lefts[at // step].wait()
            first = jnp.dot(lefts[at : at + step, :], whole, preferred_element_type=F32).astype(BF16)
            if at == 0:
                get_right.wait()
            value = jnp.dot(first, rights[...], preferred_element_type=F32)
            shaped[at : at + step, :] = value
            total = total + jnp.sum((value * value).reshape(step // 8, 8, block), axis=0)
        powers = wide(received[:, :, 2 * tiles])
        row = lax.broadcasted_iota(jnp.int32, powers.shape, 2)
        power = jnp.sum(jnp.where(row == ids[1], powers, 0.0).reshape(-1, 8, LANES), axis=0)
        scale = jnp.sqrt(jnp.sum(power, keepdims=True)) * lax.rsqrt(jnp.sum(total, keepdims=True) + NORM_EPS)
        owned = ids[0] > 0
        for at in range(0, block, step):
            here = pl.ds(at, step)

            @pl.when(owned)
            def _():
                results[here] = (shaped[here] * scale).astype(BF16)

            @pl.when(jnp.logical_not(owned))
            def _():
                results[here] = jnp.zeros((step, block), BF16)

            pltpu.make_async_copy(results.at[here], out.at[0, here], sem.at[3]).start()
        pltpu.make_async_copy(results, out.at[0], sem.at[3]).wait()

    anywhere = pl.BlockSpec(memory_space=pl.ANY)
    return call(
        kernel,
        jax.ShapeDtypeStruct((1, block, block), BF16),
        (1,),
        [pl.BlockSpec(memory_space=pltpu.VMEM), anywhere, anywhere],
        anywhere,
        [
            pltpu.VMEM((2, dp_count, 2, rows, block), BF16),
            pltpu.VMEM((block, block), BF16),
            pltpu.VMEM((block, block), BF16),
            pltpu.VMEM((block, block), F32),
            pltpu.VMEM((block, block), BF16),
            pltpu.SemaphoreType.DMA((4,)),
        ],
        cost=1 << 20,
        grant=24 * 1024 * 1024,
    )(ids, in_vmem(received), left_root, right_root)


def slot_blocks(block_owner, slot_count):
    numbers = jnp.arange(block_owner.shape[0], dtype=jnp.int32)
    queries = jnp.arange(slot_count, dtype=jnp.int32)
    matches = (queries[:, None] == block_owner[None, :]).astype(jnp.int32)
    return jnp.sum(matches * numbers[None, :], axis=1), jnp.sum(matches, axis=1)


def shards(grad_parts, moment, left_roots, right_roots, block_owner):
    dp_count = lax.axis_size("dp")
    dp_index = lax.axis_index("dp")
    matrices = grad_parts.shape[1]
    width = grad_parts.shape[3]
    block = left_roots.shape[1]
    sides = width // block
    rows = moment.shape[1] // CHUNKS
    x, y = dp_index // SIDE, dp_index % SIDE
    z, core = lax.axis_index("z"), lax.axis_index("core")
    ids = jnp.stack([jnp.where(core == 0, x, y), jnp.where(core == 0, y, x), core]).astype(jnp.int32)
    parts = grad_parts.reshape(matrices, dp_count, CHUNKS, rows, width)
    parts = pltpu.with_memory_space_constraint(parts, pltpu.HBM)
    known = moment.reshape(matrices, CHUNKS, rows, width)

    block_of, present = slot_blocks(block_owner, dp_count * SIDE * 2)
    of_plane = lax.dynamic_slice_in_dim(block_of.reshape(dp_count, SIDE, 2), z, 1, 1).reshape(-1)
    column = of_plane // (sides * sides) * sides + of_plane % sides
    plane = of_plane // sides % SIDE
    picks = jnp.stack([(plane - z) % SIDE, column], axis=1).reshape(-1)
    mine = device_number(x, y, z, core)
    own_block = block_of[mine]
    owned = jnp.stack([present[mine], own_block // (sides * sides) * sides + own_block % sides])

    def along(phase, up, down):
        return send(down, in_plane(phase, -1)), send(up, in_plane(phase, 1))

    def second_axis(mine, up, far, down):
        return [mine, send(down, in_plane(1, -1)), send(up, in_plane(1, 1)), send(far, in_plane(1, 2))]

    last = ()
    sent, own, late, sums = [], [], [], []
    for chunk in range(CHUNKS):
        up, down = extract(ids, parts, chunk, ((2, 1), (1, 0), (-2, 0), (-1, 1)), last)
        last = (up,)
        sent.append(along(0, up, down))
    for chunk in range(CHUNKS):
        own.append(extract(ids, parts, chunk, ((1, 1), (0, 0), (-1, 0), (0, 1)), last))
        last = (own[chunk][0],)
    for chunk in range(CHUNKS):
        up, down = relay(ids, *own[chunk], *sent[chunk], last)
        last = (up,)
        late.append(along(0, up, down))
    for chunk in range(CHUNKS):
        terms = first_sum(ids, *own[chunk], *sent[chunk], *late[chunk], last)
        last = (terms[0],)
        sums.append(second_axis(*terms))
    held = []
    power = []
    for chunk in range(CHUNKS):
        pieces, *power = second_sum(ids, sums[chunk], known, chunk, block, power, last)
        last = (pieces,)
        held.append([pieces] + [send(pieces, lambda core, k=k: (0, 0, -k, 0)) for k in (1, 2, 3)])
    outgoing = choose(picks, held, last)
    received = lax.all_to_all(outgoing, ("dp", "core"), 0, 0, tiled=True)
    received = received.reshape((dp_count, 2) + received.shape[1:])
    left, right = (pltpu.with_memory_space_constraint(value, pltpu.HBM) for value in (left_roots, right_roots))
    return finish(owned, received, left, right, block)


def solution(mesh):
    split = jax.sharding.Mesh(mesh.devices.reshape(-1, SIDE, 2), ("dp", "z", "core"))
    placed = (
        P("dp", None, ("z", "core"), None),
        P(None, ("z", "core", "dp"), None),
        P(("dp", "z", "core"), None, None),
        P(("dp", "z", "core"), None, None),
        P(),
    )
    return jax.shard_map(
        shards, mesh=split, in_specs=placed, out_specs=P(("dp", "z", "core"), None, None), check_vma=False
    )
```

```python
import jax
import jax.numpy as jnp
from jax import lax
from jax.experimental import pallas as pl
from jax.experimental.pallas import tpu as pltpu
from jax.sharding import PartitionSpec as P

BETA_TWO = 0.999
ADAM_EPS = 1e-08
NORM_EPS = 1e-06
SIDE = 4
CHUNKS = 2
LANES = 128
PIECES = 12
VMEM_LIMIT = 12 * 1024 * 1024
VMEM_MOST = 20 * 1024 * 1024
F32 = jnp.float32
BF16 = jnp.bfloat16


def device_number(x, y, z, core):
    return ((x * SIDE + y) * SIDE + z) * 2 + core


def routes(move):
    pairs = []
    for x in range(SIDE):
        for y in range(SIDE):
            for z in range(SIDE):
                for core in range(2):
                    dx, dy, dz, swap = move(core)
                    target = device_number((x + dx) % SIDE, (y + dy) % SIDE, (z + dz) % SIDE, core ^ swap)
                    pairs.append((device_number(x, y, z, core), target))
    return pairs


def send(value, move):
    return lax.ppermute(value, ("dp", "z", "core"), routes(move))


def in_plane(phase, sign):
    return lambda core: (sign, 0, 0, 0) if core == phase else (0, sign, 0, 0)


def wide(value):
    return value.astype(F32)


def in_vmem(value):
    return pltpu.with_memory_space_constraint(value, pltpu.VMEM)


def call(kernel, out_shape, grid, in_specs, out_specs, scratch=(), cost=1, after=(), grant=VMEM_MOST):
    inputs = len(in_specs)
    in_specs = list(in_specs) + [pl.BlockSpec(memory_space=pl.ANY)] * len(after)

    def body(ids, *refs):
        kernel(ids, *refs[:inputs], *refs[len(in_specs) :])

    made = pl.pallas_call(
        body,
        out_shape=out_shape,
        grid_spec=pltpu.PrefetchScalarGridSpec(
            num_scalar_prefetch=1, grid=grid, in_specs=in_specs, out_specs=out_specs, scratch_shapes=list(scratch)
        ),
        compiler_params=pltpu.CompilerParams(vmem_limit_bytes=grant),
        cost_estimate=pl.CostEstimate(flops=cost, bytes_accessed=4 * cost, transcendentals=0),
    )
    return lambda *operands: made(*operands, *after)


def row_block(ids, j, q):
    j, q = lax.rem(j + 2 * SIDE, SIDE), lax.rem(q + 2 * SIDE, SIDE)
    return jnp.where(ids[2] == 0, j * SIDE + q, q * SIDE + j)


def extract(ids, parts, chunk, pieces, after):
    m, _, _, rows, width = parts.shape
    half = width // 2
    count = len(pieces) // 2

    def kernel(ids, source, up, down, sem):
        copies = []
        for number, (offset, column) in enumerate(pieces):
            out, part = (up, down)[number // count], number % count
            for q in range(SIDE):
                block = row_block(ids, ids[0] + offset, q)
                place = source.at[:, block, chunk, :, pl.ds(column * half, half)]
                copies.append(pltpu.make_async_copy(place, out.at[part, :, q], sem.at[number, q]))
        for copy in copies:
            copy.start()
        for copy in copies:
            copy.wait()

    here = pl.BlockSpec(memory_space=pltpu.VMEM)
    return call(
        kernel,
        [pltpu.VMEM((count, m, SIDE, rows, half), BF16)] * 2,
        (1,),
        [pl.BlockSpec(memory_space=pl.ANY)],
        [here, here],
        [pltpu.SemaphoreType.DMA((2 * count, SIDE))],
        after=after,
    )(ids, parts)


def relay(ids, own_up, own_down, from_up, from_down, after):
    _, m, _, rows, half = own_up.shape

    def kernel(ids, a, b, below, above, up, down):
        q = pl.program_id(0)
        up[:, q] = (wide(a[0, :, q]) + wide(below[0, :, q])).astype(BF16)
        down[:, q] = (wide(b[0, :, q]) + wide(above[0, :, q])).astype(BF16)

    here = pl.BlockSpec(memory_space=pltpu.VMEM)
    return call(
        kernel,
        [pltpu.VMEM((m, SIDE, rows, half), BF16)] * 2,
        (SIDE,),
        [here] * 4,
        [here, here],
        after=after,
    )(ids, *(in_vmem(value) for value in (own_up, own_down, from_down, from_up)))


def first_sum(ids, own_up, own_down, from_up, from_down, late_up, late_down, after):
    _, m, _, rows, half = own_up.shape

    def kernel(ids, own_left, own_right, below, above, late_above, late_below, mine, *others):
        t = pl.program_id(0)
        q = lax.rem(ids[1] + 1 + t, SIDE)
        left = (wide(own_left[1, :, q]) + wide(below[1, :, q]) + wide(late_above[:, q])).astype(BF16)
        right = (wide(own_right[1, :, q]) + wide(above[1, :, q]) + wide(late_below[:, q])).astype(BF16)
        for number, out in enumerate((*others, mine)):

            @pl.when(t == number)
            def _(out=out):
                out[:, :, :half] = left
                out[:, :, half:] = right

    here = pl.BlockSpec(memory_space=pltpu.VMEM)
    return call(
        kernel,
        [pltpu.VMEM((m, rows, 2 * half), BF16)] * SIDE,
        (SIDE,),
        [here] * 6,
        [here] * SIDE,
        after=after,
    )(ids, *(in_vmem(value) for value in (own_up, own_down, from_down, from_up, late_up, late_down)))


def second_sum(ids, sums, moment, chunk, block, earlier, after):
    m, rows, width = sums[0].shape
    sides = width // block
    tiles = block // LANES
    last = len(earlier) > 0

    def kernel(ids, *refs):
        terms, known = refs[: len(sums)], refs[len(sums)]
        t = pl.program_id(0)
        if last:
            before, out, powers = refs[len(sums) + 1 :]
        else:
            out, powers = refs[len(sums) + 1 :]
        for side in range(sides):
            power = before[side] if last else jnp.zeros((rows, LANES), F32)
            for tile in range(tiles):
                at = pl.ds(side * block + tile * LANES, LANES)
                gradient = sum(wide(term[0, :, at]) for term in terms)
                second = BETA_TWO * known[0, 0, :, at] + (1.0 - BETA_TWO) * gradient * gradient
                direction = gradient / (jnp.sqrt(second) + ADAM_EPS)
                power = power + direction * direction
                out[(t * sides + side) * tiles + tile] = gradient.astype(BF16)
            if last:
                row = lax.broadcasted_iota(jnp.int32, (rows, LANES), 0)
                placed = jnp.where(row == t * sides + side, jnp.sum(power, axis=0, keepdims=True), 0.0)
                powers[...] = jnp.where(t + side == 0, 0.0, powers[...]) + placed
            else:
                powers[side] = power
        if last:

            @pl.when(t == m - 1)
            def _():
                out[m * sides * tiles] = powers[...].astype(BF16)

    power_spec = pl.BlockSpec((sides, rows, LANES), lambda t, ids: (t, 0, 0))
    shapes = [jax.ShapeDtypeStruct((m * sides * tiles + last, rows, LANES), BF16)]
    specs = [pl.BlockSpec((m * sides * tiles + last, rows, LANES), lambda t, ids: (0, 0, 0))]
    if not last:
        shapes.append(jax.ShapeDtypeStruct((m * sides, rows, LANES), F32))
        specs.append(power_spec)
    return call(
        kernel,
        shapes,
        (m,),
        [pl.BlockSpec((1, rows, width), lambda t, ids: (t, 0, 0))] * len(sums)
        + [pl.BlockSpec((1, 1, rows, width), lambda t, ids: (t, chunk, 0, 0))]
        + [power_spec] * len(earlier),
        specs,
        [pltpu.VMEM((rows, LANES), F32)] * last,
        after=after,
        grant=VMEM_LIMIT,
    )(ids, *sums, moment, *earlier)


def choose(picks, held, after):
    slots = picks.shape[0] // 2
    count = len(held[0])
    total, rows, _ = held[0][0].shape
    tiles = total // PIECES

    def kernel(picks, *refs):
        first, second, out, staged, sem = refs[:count], refs[count : 2 * count], *refs[2 * count :]

        @pl.loop(0, slots)
        def _(slot):
            piece = pl.ds(picks[2 * slot + 1] * tiles, tiles)
            for number in range(count):

                @pl.when(picks[2 * slot] == number)
                def _(number=number):
                    staged[slot, :tiles] = first[number][piece]
                    staged[slot, tiles : 2 * tiles] = second[number][piece]
                    staged[slot, 2 * tiles] = second[number][total]

            pltpu.make_async_copy(staged.at[slot], out.at[slot], sem).start()

        pltpu.make_async_copy(staged, out, sem).wait()

    shape = (slots, 2 * tiles + 1, rows, LANES)
    return call(
        kernel,
        jax.ShapeDtypeStruct(shape, BF16),
        (1,),
        [pl.BlockSpec(memory_space=pltpu.VMEM)] * (2 * count),
        pl.BlockSpec(memory_space=pl.ANY),
        [pltpu.VMEM(shape, BF16), pltpu.SemaphoreType.DMA],
        after=after,
        grant=VMEM_LIMIT,
    )(picks, *(in_vmem(value) for value in (*held[0], *held[1])))


def finish(ids, received, left_root, right_root, block):
    dp_count, _, _, rows, _ = received.shape
    tiles = block // LANES
    step, part = block // 2, block // 4

    def kernel(ids, received, left, right, out, grads, lefts, rights, shaped, results, sem):
        get_lefts = [
            pltpu.make_async_copy(left.at[0, pl.ds(at, step)], lefts.at[pl.ds(at, step)], sem.at[at // step])
            for at in range(0, block, step)
        ]
        get_right = pltpu.make_async_copy(right.at[0], rights, sem.at[2])
        get_lefts[0].start()
        get_right.start()
        for get in get_lefts[1:]:
            get.start()

        @pl.loop(0, dp_count)
        def _(group):
            for core in range(2):
                for tile in range(2 * tiles):
                    columns = slice(tile % tiles * LANES, (tile % tiles + 1) * LANES)
                    grads[core, group, tile // tiles, :, columns] = received[group, core, tile]

        total = jnp.zeros((8, block), F32)
        for at in range(0, block, step):
            whole = grads[...].reshape(block, block)
            get_lefts[at // step].wait()
            first = jnp.dot(lefts[at : at + step, :], whole, preferred_element_type=F32).astype(BF16)
            if at == 0:
                get_right.wait()
            value = jnp.dot(first, rights[...], preferred_element_type=F32)
            shaped[at : at + step, :] = value
            total = total + jnp.sum((value * value).reshape(step // 8, 8, block), axis=0)
        powers = wide(received[:, :, 2 * tiles])
        row = lax.broadcasted_iota(jnp.int32, powers.shape, 2)
        power = jnp.sum(jnp.where(row == ids[1], powers, 0.0).reshape(-1, 8, LANES), axis=0)
        scale = jnp.sqrt(jnp.sum(power, keepdims=True)) * lax.rsqrt(jnp.sum(total, keepdims=True) + NORM_EPS)
        owned = ids[0] > 0
        for at in range(0, block, part):
            here = pl.ds(at, part)

            @pl.when(owned)
            def _():
                results[here] = (shaped[here] * scale).astype(BF16)

            @pl.when(jnp.logical_not(owned))
            def _():
                results[here] = jnp.zeros((part, block), BF16)

            pltpu.make_async_copy(results.at[here], out.at[0, here], sem.at[3]).start()
        pltpu.make_async_copy(results, out.at[0], sem.at[3]).wait()

    anywhere = pl.BlockSpec(memory_space=pl.ANY)
    return call(
        kernel,
        jax.ShapeDtypeStruct((1, block, block), BF16),
        (1,),
        [pl.BlockSpec(memory_space=pltpu.VMEM), anywhere, anywhere],
        anywhere,
        [
            pltpu.VMEM((2, dp_count, 2, rows, block), BF16),
            pltpu.VMEM((block, block), BF16),
            pltpu.VMEM((block, block), BF16),
            pltpu.VMEM((block, block), F32),
            pltpu.VMEM((block, block), BF16),
            pltpu.SemaphoreType.DMA((4,)),
        ],
        cost=1 << 20,
        grant=24 * 1024 * 1024,
    )(ids, in_vmem(received), left_root, right_root)


def slot_blocks(block_owner, slot_count):
    numbers = jnp.arange(block_owner.shape[0], dtype=jnp.int32)
    queries = jnp.arange(slot_count, dtype=jnp.int32)
    matches = (queries[:, None] == block_owner[None, :]).astype(jnp.int32)
    return jnp.sum(matches * numbers[None, :], axis=1), jnp.sum(matches, axis=1)


def shards(grad_parts, moment, left_roots, right_roots, block_owner):
    dp_count = lax.axis_size("dp")
    dp_index = lax.axis_index("dp")
    matrices = grad_parts.shape[1]
    width = grad_parts.shape[3]
    block = left_roots.shape[1]
    sides = width // block
    rows = moment.shape[1] // CHUNKS
    x, y = dp_index // SIDE, dp_index % SIDE
    z, core = lax.axis_index("z"), lax.axis_index("core")
    ids = jnp.stack([jnp.where(core == 0, x, y), jnp.where(core == 0, y, x), core]).astype(jnp.int32)
    parts = grad_parts.reshape(matrices, dp_count, CHUNKS, rows, width)
    parts = pltpu.with_memory_space_constraint(parts, pltpu.HBM)
    known = moment.reshape(matrices, CHUNKS, rows, width)

    block_of, present = slot_blocks(block_owner, dp_count * SIDE * 2)
    of_plane = lax.dynamic_slice_in_dim(block_of.reshape(dp_count, SIDE, 2), z, 1, 1).reshape(-1)
    column = of_plane // (sides * sides) * sides + of_plane % sides
    plane = of_plane // sides % SIDE
    picks = jnp.stack([(plane - z) % SIDE, column], axis=1).reshape(-1)
    mine = device_number(x, y, z, core)
    own_block = block_of[mine]
    owned = jnp.stack([present[mine], own_block // (sides * sides) * sides + own_block % sides])

    def along(phase, up, down):
        return send(down, in_plane(phase, -1)), send(up, in_plane(phase, 1))

    def second_axis(mine, up, far, down):
        return [mine, send(down, in_plane(1, -1)), send(up, in_plane(1, 1)), send(far, in_plane(1, 2))]

    last = ()
    sent, own, late, sums = [], [], [], []
    for chunk in range(CHUNKS):
        up, down = extract(ids, parts, chunk, ((2, 1), (1, 0), (-2, 0), (-1, 1)), last)
        last = (up,)
        sent.append(along(0, up, down))
    for chunk in range(CHUNKS):
        own.append(extract(ids, parts, chunk, ((1, 1), (0, 0), (-1, 0), (0, 1)), last))
        last = (own[chunk][0],)
    for chunk in range(CHUNKS):
        up, down = relay(ids, *own[chunk], *sent[chunk], last)
        last = (up,)
        late.append(along(0, up, down))
    for chunk in range(CHUNKS):
        terms = first_sum(ids, *own[chunk], *sent[chunk], *late[chunk], last)
        last = (terms[0],)
        sums.append(second_axis(*terms))
    held = []
    power = []
    for chunk in range(CHUNKS):
        pieces, *power = second_sum(ids, sums[chunk], known, chunk, block, power, last)
        last = (pieces,)
        held.append([pieces] + [send(pieces, lambda core, k=k: (0, 0, -k, 0)) for k in (1, 2, 3)])
    outgoing = choose(picks, held, last)
    received = lax.all_to_all(outgoing, ("dp", "core"), 0, 0, tiled=True)
    received = received.reshape((dp_count, 2) + received.shape[1:])
    left, right = (pltpu.with_memory_space_constraint(value, pltpu.HBM) for value in (left_roots, right_roots))
    return finish(owned, received, left, right, block)


def solution(mesh):
    split = jax.sharding.Mesh(mesh.devices.reshape(-1, SIDE, 2), ("dp", "z", "core"))
    placed = (
        P("dp", None, ("z", "core"), None),
        P(None, ("z", "core", "dp"), None),
        P(("dp", "z", "core"), None, None),
        P(("dp", "z", "core"), None, None),
        P(),
    )
    return jax.shard_map(
        shards, mesh=split, in_specs=placed, out_specs=P(("dp", "z", "core"), None, None), check_vma=False
    )
```

```python
import jax
import jax.numpy as jnp
from jax import lax
from jax.experimental import pallas as pl
from jax.experimental.pallas import tpu as pltpu
from jax.sharding import PartitionSpec as P

BETA_TWO = 0.999
ADAM_EPS = 1e-08
NORM_EPS = 1e-06
SIDE = 4
CHUNKS = 2
LANES = 128
TILES = 17
PIECES = 12
VMEM_LIMIT = 12 * 1024 * 1024
VMEM_MOST = 20 * 1024 * 1024
F32 = jnp.float32
BF16 = jnp.bfloat16


def device_number(x, y, z, core):
    return ((x * SIDE + y) * SIDE + z) * 2 + core


def routes(move):
    pairs = []
    for x in range(SIDE):
        for y in range(SIDE):
            for z in range(SIDE):
                for core in range(2):
                    dx, dy, dz, swap = move(core)
                    target = device_number((x + dx) % SIDE, (y + dy) % SIDE, (z + dz) % SIDE, core ^ swap)
                    pairs.append((device_number(x, y, z, core), target))
    return pairs


def send(value, move):
    return lax.ppermute(value, ("dp", "z", "core"), routes(move))


def in_plane(phase, sign):
    return lambda core: (sign, 0, 0, 0) if core == phase else (0, sign, 0, 0)


def wide(value):
    return value.astype(F32)


def in_vmem(value):
    return pltpu.with_memory_space_constraint(value, pltpu.VMEM)


def call(kernel, out_shape, grid, in_specs, out_specs, scratch=(), cost=1, after=(), grant=VMEM_MOST, aliases=()):
    inputs = len(in_specs)
    in_specs = list(in_specs) + [pl.BlockSpec(memory_space=pl.ANY)] * len(after)

    def body(ids, *refs):
        kernel(ids, *refs[:inputs], *refs[len(in_specs) :])

    made = pl.pallas_call(
        body,
        out_shape=out_shape,
        grid_spec=pltpu.PrefetchScalarGridSpec(
            num_scalar_prefetch=1, grid=grid, in_specs=in_specs, out_specs=out_specs, scratch_shapes=list(scratch)
        ),
        input_output_aliases=dict(aliases),
        compiler_params=pltpu.CompilerParams(vmem_limit_bytes=grant),
        cost_estimate=pl.CostEstimate(flops=cost, bytes_accessed=4 * cost, transcendentals=0),
    )
    return lambda *operands: made(*operands, *after)


def row_block(ids, j, q):
    j, q = lax.rem(j + 2 * SIDE, SIDE), lax.rem(q + 2 * SIDE, SIDE)
    return jnp.where(ids[2] == 0, j * SIDE + q, q * SIDE + j)


def extract(ids, parts, chunk, pieces, after):
    m, _, _, rows, width = parts.shape
    half = width // 2
    count = len(pieces) // 2

    def kernel(ids, source, up, down, sem):
        copies = []
        for number, (offset, column) in enumerate(pieces):
            out, part = (up, down)[number // count], number % count
            for q in range(SIDE):
                block = row_block(ids, ids[0] + offset, q)
                place = source.at[:, block, chunk, :, pl.ds(column * half, half)]
                copies.append(pltpu.make_async_copy(place, out.at[part, :, q], sem.at[number, q]))
        for copy in copies:
            copy.start()
        for copy in copies:
            copy.wait()

    here = pl.BlockSpec(memory_space=pltpu.VMEM)
    return call(
        kernel,
        [pltpu.VMEM((count, m, SIDE, rows, half), BF16)] * 2,
        (1,),
        [pl.BlockSpec(memory_space=pl.ANY)],
        [here, here],
        [pltpu.SemaphoreType.DMA((2 * count, SIDE))],
        after=after,
    )(ids, parts)


def relay(ids, own_up, own_down, from_up, from_down, after):
    _, m, _, rows, half = own_up.shape

    def kernel(ids, a, b, below, above, up, down):
        q = pl.program_id(0)
        up[:, q] = (wide(a[0, :, q]) + wide(below[0, :, q])).astype(BF16)
        down[:, q] = (wide(b[0, :, q]) + wide(above[0, :, q])).astype(BF16)

    here = pl.BlockSpec(memory_space=pltpu.VMEM)
    return call(
        kernel,
        [pltpu.VMEM((m, SIDE, rows, half), BF16)] * 2,
        (SIDE,),
        [here] * 4,
        [here, here],
        after=after,
    )(ids, *(in_vmem(value) for value in (own_up, own_down, from_down, from_up)))


def first_sum(ids, own_up, own_down, from_up, from_down, late_up, late_down, after):
    _, m, _, rows, half = own_up.shape

    def kernel(ids, own_left, own_right, below, above, late_above, late_below, mine, *others):
        t = pl.program_id(0)
        q = lax.rem(ids[1] + 1 + t, SIDE)
        left = (wide(own_left[1, :, q]) + wide(below[1, :, q]) + wide(late_above[:, q])).astype(BF16)
        right = (wide(own_right[1, :, q]) + wide(above[1, :, q]) + wide(late_below[:, q])).astype(BF16)
        for number, out in enumerate((*others, mine)):

            @pl.when(t == number)
            def _(out=out):
                out[:, :, :half] = left
                out[:, :, half:] = right

    here = pl.BlockSpec(memory_space=pltpu.VMEM)
    return call(
        kernel,
        [pltpu.VMEM((m, rows, 2 * half), BF16)] * SIDE,
        (SIDE,),
        [here] * 6,
        [here] * SIDE,
        after=after,
    )(ids, *(in_vmem(value) for value in (own_up, own_down, from_down, from_up, late_up, late_down)))


def second_sum(ids, sums, moment, chunk, block, earlier, after):
    m, rows, width = sums[0].shape
    sides = width // block
    tiles = block // LANES
    last = len(earlier) > 0

    def kernel(ids, *refs):
        terms, known = refs[: len(sums)], refs[len(sums)]
        t = pl.program_id(0)
        if last:
            before, out, powers = refs[len(sums) + 1 :]
        else:
            out, powers = refs[len(sums) + 1 :]
        for side in range(sides):
            power = before[side] if last else jnp.zeros((rows, LANES), F32)
            for tile in range(tiles):
                at = pl.ds(side * block + tile * LANES, LANES)
                gradient = sum(wide(term[0, :, at]) for term in terms)
                second = BETA_TWO * known[0, 0, :, at] + (1.0 - BETA_TWO) * gradient * gradient
                direction = gradient / (jnp.sqrt(second) + ADAM_EPS)
                power = power + direction * direction
                out[(t * sides + side) * tiles + tile] = gradient.astype(BF16)
            if last:
                row = lax.broadcasted_iota(jnp.int32, (rows, LANES), 0)
                placed = jnp.where(row == t * sides + side, jnp.sum(power, axis=0, keepdims=True), 0.0)
                powers[...] = jnp.where(t + side == 0, 0.0, powers[...]) + placed
            else:
                powers[side] = power
        if last:

            @pl.when(t == m - 1)
            def _():
                out[m * sides * tiles] = powers[...].astype(BF16)

    power_spec = pl.BlockSpec((sides, rows, LANES), lambda t, ids: (t, 0, 0))
    shapes = [jax.ShapeDtypeStruct((m * sides * tiles + last, rows, LANES), BF16)]
    specs = [pl.BlockSpec((m * sides * tiles + last, rows, LANES), lambda t, ids: (0, 0, 0))]
    if not last:
        shapes.append(jax.ShapeDtypeStruct((m * sides, rows, LANES), F32))
        specs.append(power_spec)
    return call(
        kernel,
        shapes,
        (m,),
        [pl.BlockSpec((1, rows, width), lambda t, ids: (t, 0, 0))] * len(sums)
        + [pl.BlockSpec((1, 1, rows, width), lambda t, ids: (t, chunk, 0, 0))]
        + [power_spec] * len(earlier),
        specs,
        [pltpu.VMEM((rows, LANES), F32)] * last,
        after=after,
        grant=VMEM_LIMIT,
    )(ids, *sums, moment, *earlier)


def choose(picks, held, filled, start, after):
    slots = picks.shape[0] // 2
    total, rows, _ = held[0].shape
    tiles, extra = divmod(total, PIECES)

    def kernel(picks, *refs):
        sources, (out, staged, sem) = refs[: len(held)], refs[-3:]

        @pl.loop(0, slots, unroll=4)
        def _(slot):
            piece = pl.ds(picks[2 * slot + 1] * tiles, tiles)
            for number, source in enumerate(sources):

                @pl.when(picks[2 * slot] == number)
                def _(source=source):
                    staged[slot, :tiles] = source[piece]
                    if extra:
                        staged[slot, tiles] = source[total - 1]

            pltpu.make_async_copy(staged.at[slot], out.at[slot, pl.ds(start, tiles + extra)], sem).start()

        pltpu.make_async_copy(staged, out.at[:, pl.ds(start, tiles + extra)], sem).wait()

    anywhere = pl.BlockSpec(memory_space=pl.ANY)
    return call(
        kernel,
        jax.ShapeDtypeStruct((slots, TILES, rows, LANES), BF16),
        (1,),
        [pl.BlockSpec(memory_space=pltpu.VMEM)] * len(held) + [anywhere] * len(filled),
        anywhere,
        [pltpu.VMEM((slots, tiles + extra, rows, LANES), BF16), pltpu.SemaphoreType.DMA],
        after=after,
        grant=VMEM_LIMIT,
        aliases=[(1 + len(held), 0)] if filled else (),
    )(picks, *(in_vmem(value) for value in held), *filled)


def finish(ids, received, left_root, right_root, block):
    dp_count, _, _, rows, _ = received.shape
    tiles = block // LANES
    step, part = block // 2, block // 4

    def kernel(ids, received, left, right, out, grads, lefts, rights, shaped, results, sem):
        get_lefts = [
            pltpu.make_async_copy(left.at[0, pl.ds(at, step)], lefts.at[pl.ds(at, step)], sem.at[at // step])
            for at in range(0, block, step)
        ]
        get_right = pltpu.make_async_copy(right.at[0], rights, sem.at[2])
        get_lefts[0].start()
        get_right.start()
        for get in get_lefts[1:]:
            get.start()

        @pl.loop(0, dp_count)
        def _(group):
            for core in range(2):
                for tile in range(2 * tiles):
                    columns = slice(tile % tiles * LANES, (tile % tiles + 1) * LANES)
                    grads[core, group, tile // tiles, :, columns] = received[group, core, tile]

        total = jnp.zeros((8, block), F32)
        for at in range(0, block, step):
            whole = grads[...].reshape(block, block)
            get_lefts[at // step].wait()
            first = jnp.dot(lefts[at : at + step, :], whole, preferred_element_type=F32).astype(BF16)
            if at == 0:
                get_right.wait()
            value = jnp.dot(first, rights[...], preferred_element_type=F32)
            shaped[at : at + step, :] = value
            total = total + jnp.sum((value * value).reshape(step // 8, 8, block), axis=0)
        powers = wide(received[:, :, 2 * tiles])
        row = lax.broadcasted_iota(jnp.int32, powers.shape, 2)
        power = jnp.sum(jnp.where(row == ids[1], powers, 0.0).reshape(-1, 8, LANES), axis=0)
        scale = jnp.sqrt(jnp.sum(power, keepdims=True)) * lax.rsqrt(jnp.sum(total, keepdims=True) + NORM_EPS)
        owned = ids[0] > 0
        for at in range(0, block, part):
            here = pl.ds(at, part)

            @pl.when(owned)
            def _():
                results[here] = (shaped[here] * scale).astype(BF16)

            @pl.when(jnp.logical_not(owned))
            def _():
                results[here] = jnp.zeros((part, block), BF16)

            pltpu.make_async_copy(results.at[here], out.at[0, here], sem.at[3]).start()
        pltpu.make_async_copy(results, out.at[0], sem.at[3]).wait()

    anywhere = pl.BlockSpec(memory_space=pl.ANY)
    return call(
        kernel,
        jax.ShapeDtypeStruct((1, block, block), BF16),
        (1,),
        [pl.BlockSpec(memory_space=pltpu.VMEM), anywhere, anywhere],
        anywhere,
        [
            pltpu.VMEM((2, dp_count, 2, rows, block), BF16),
            pltpu.VMEM((block, block), BF16),
            pltpu.VMEM((block, block), BF16),
            pltpu.VMEM((block, block), F32),
            pltpu.VMEM((block, block), BF16),
            pltpu.SemaphoreType.DMA((4,)),
        ],
        cost=1 << 20,
        grant=24 * 1024 * 1024,
    )(ids, in_vmem(received), left_root, right_root)


def slot_blocks(block_owner, slot_count):
    numbers = jnp.arange(block_owner.shape[0], dtype=jnp.int32)
    queries = jnp.arange(slot_count, dtype=jnp.int32)
    matches = (queries[:, None] == block_owner[None, :]).astype(jnp.int32)
    return jnp.sum(matches * numbers[None, :], axis=1), jnp.sum(matches, axis=1)


def shards(grad_parts, moment, left_roots, right_roots, block_owner):
    dp_count = lax.axis_size("dp")
    dp_index = lax.axis_index("dp")
    matrices = grad_parts.shape[1]
    width = grad_parts.shape[3]
    block = left_roots.shape[1]
    sides = width // block
    rows = moment.shape[1] // CHUNKS
    x, y = dp_index // SIDE, dp_index % SIDE
    z, core = lax.axis_index("z"), lax.axis_index("core")
    ids = jnp.stack([jnp.where(core == 0, x, y), jnp.where(core == 0, y, x), core]).astype(jnp.int32)
    parts = grad_parts.reshape(matrices, dp_count, CHUNKS, rows, width)
    parts = pltpu.with_memory_space_constraint(parts, pltpu.HBM)
    known = moment.reshape(matrices, CHUNKS, rows, width)

    block_of, present = slot_blocks(block_owner, dp_count * SIDE * 2)
    of_plane = lax.dynamic_slice_in_dim(block_of.reshape(dp_count, SIDE, 2), z, 1, 1).reshape(-1)
    column = of_plane // (sides * sides) * sides + of_plane % sides
    plane = of_plane // sides % SIDE
    picks = jnp.stack([(plane - z) % SIDE, column], axis=1).reshape(-1)
    mine = device_number(x, y, z, core)
    own_block = block_of[mine]
    owned = jnp.stack([present[mine], own_block // (sides * sides) * sides + own_block % sides])

    def along(phase, up, down):
        return send(down, in_plane(phase, -1)), send(up, in_plane(phase, 1))

    def second_axis(mine, up, far, down):
        return [mine, send(down, in_plane(1, -1)), send(up, in_plane(1, 1)), send(far, in_plane(1, 2))]

    last = ()
    sent, own, late, sums = [], [], [], []
    for chunk in range(CHUNKS):
        up, down = extract(ids, parts, chunk, ((2, 1), (1, 0), (-2, 0), (-1, 1)), last)
        last = (up,)
        sent.append(along(0, up, down))
    for chunk in range(CHUNKS):
        own.append(extract(ids, parts, chunk, ((1, 1), (0, 0), (-1, 0), (0, 1)), last))
        last = (own[chunk][0],)
    for chunk in range(CHUNKS):
        up, down = relay(ids, *own[chunk], *sent[chunk], last)
        last = (up,)
        late.append(along(0, up, down))
    for chunk in range(CHUNKS):
        terms = first_sum(ids, *own[chunk], *sent[chunk], *late[chunk], last)
        last = (terms[0],)
        sums.append(second_axis(*terms))
    held = []
    power = []
    for chunk in range(CHUNKS):
        pieces, *power = second_sum(ids, sums[chunk], known, chunk, block, power, last)
        last = (pieces,)
        held.append([pieces] + [send(pieces, lambda core, k=k: (0, 0, -k, 0)) for k in (1, 2, 3)])
    outgoing = choose(picks, held[0], (), 0, last)
    outgoing = choose(picks, held[1], (outgoing,), TILES // 2, ())
    received = lax.all_to_all(outgoing, ("dp", "core"), 0, 0, tiled=True)
    received = received.reshape((dp_count, 2) + received.shape[1:])
    left, right = (pltpu.with_memory_space_constraint(value, pltpu.HBM) for value in (left_roots, right_roots))
    return finish(owned, received, left, right, block)


def solution(mesh):
    split = jax.sharding.Mesh(mesh.devices.reshape(-1, SIDE, 2), ("dp", "z", "core"))
    placed = (
        P("dp", None, ("z", "core"), None),
        P(None, ("z", "core", "dp"), None),
        P(("dp", "z", "core"), None, None),
        P(("dp", "z", "core"), None, None),
        P(),
    )
    return jax.shard_map(
        shards, mesh=split, in_specs=placed, out_specs=P(("dp", "z", "core"), None, None), check_vma=False
    )
```
